32 devices in a mesh: gx: 8 (over z, x), gy: 4 (over y, core).
Axes of the slice: x: 2, y: 2, z: 4, core: 2. Of those that a mesh axis runs over, the one named last changes fastest.
Arguments:
- particles: float32 [4, 65536], P(None, ('gx', 'gy')), may hold values from -1 to 1, as said below
- tree_cells: float32 [10, 262144], P(None, ('gx', 'gy')), may hold values from -1 to 1, as said below
- let_list: int32 [32, 32, 4], P(('gx', 'gy')), may hold values from 0 to 63
- let_count: int32 [32, 32], P(('gx', 'gy')), may hold values from 1 to 4, as said below
- part_list: int32 [32, 4, 4], P(('gx', 'gy')), may hold values from 0 to 15
- cell_lists: int32 [512, 16], P(('gx', 'gy')), may hold values from 0 to 191
- near_lists: int32 [512, 8], P(('gx', 'gy')), may hold values from 0 to 31
Outputs:
- forces: float32 [4, 65536], P(None, ('gx', 'gy'))
The draws below stay inside these ranges and needn't reach their ends.
Inputs may be any that keep to these rules, and one draw needn't show every extreme that they name: let_count is 4 wherever sender and receiver are at most 2 apart along gx+gy, and between 1 and 4 elsewhere. `particles`: positions lie in [-1, 1], masses are positive. `tree_cells`: centres lie in [-1, 1], masses are positive, the quadrupole is traceless.
All inputs are finite; a program needn't handle non-finite values.
Results may differ from the reference program's by a relative error of at most 0.0003.
Values sent between devices are 32-bit elements; how exact they have to be, the bound alone decides.
No kernel may reach another device: no remote copies, remote signals or barrier semaphores. Data moves between devices by JAX's collectives and lax.ppermute only.
A program may use at most 64 MiB of HBM per device.

```python
import math
import jax
import jax.numpy as jnp
from jax import lax

NBLK = 16
NCB = 64
BLK = 128
SLOTS = 4
BPB = 4
LC = 16
LP = 8
DEVICES = 32


def draw_particles(key, part):
    keys = jax.random.split(key, 2)
    count = NBLK * BLK * DEVICES
    centre = jax.random.uniform(keys[0], (3, count), jnp.float32, -1.0, 1.0)
    masses = jnp.exp(jax.random.uniform(keys[1], (1, count), jnp.float32, math.log(0.0001), math.log(0.001)))
    return jnp.concatenate([centre, masses], axis=0)


def draw_tree_cells(key, part):
    keys = jax.random.split(key, 3)
    count = NCB * BLK * DEVICES
    centre = jax.random.uniform(keys[0], (3, count), jnp.float32, -1.0, 1.0)
    masses = jnp.exp(jax.random.uniform(keys[1], (1, count), jnp.float32, math.log(0.0005), math.log(0.005)))
    shape_terms = jax.random.normal(keys[2], (5, count), jnp.float32) * 0.08 * masses
    quad_xx = shape_terms[0:1]
    quad_yy = shape_terms[1:2]
    quad_zz = -(quad_xx + quad_yy)
    return jnp.concatenate([centre, masses, quad_xx, quad_yy, quad_zz, shape_terms[2:5]], axis=0)


def draw_let_count(key, part):
    senders = jnp.arange(DEVICES, dtype=jnp.int32)[:, None]
    receivers = jnp.arange(DEVICES, dtype=jnp.int32)[None, :]
    nearby = jnp.abs(senders - receivers) <= 2
    farther = jax.random.randint(key, (DEVICES, DEVICES), 1, SLOTS + 1, dtype=jnp.int32)
    return jnp.where(nearby, jnp.int32(SLOTS), farther).astype(jnp.int32)


def set_ends(values, stream_key, least, high):
    longest = values.shape.index(max(values.shape))
    spots = []
    for shift in (0, 1):
        where = [jax.random.randint(jax.random.fold_in(stream_key, axis), (), 0, length) for axis, length in enumerate(values.shape)]
        where[longest] = (where[longest] + shift) % values.shape[longest]
        spots.append(tuple(where))
    return values.at[spots[0]].set(least).at[spots[1]].set(high)


def setup_inputs(seed: int = 0) -> dict:
    streams_of = jax.random.split(jax.random.key(seed), 8)
    particles = draw_particles(jax.random.fold_in(streams_of[7], 71), 0)
    tree_cells = draw_tree_cells(jax.random.fold_in(streams_of[7], 71), 0)
    let_list = set_ends(jax.random.randint(streams_of[2], (DEVICES, DEVICES, SLOTS), 0, NCB), jax.random.fold_in(streams_of[2], 1), 0, NCB - 1).astype(jnp.int32)
    let_count = draw_let_count(jax.random.fold_in(streams_of[7], 71), 0)
    part_list = set_ends(jax.random.randint(streams_of[4], (DEVICES, 4, BPB), 0, NBLK), jax.random.fold_in(streams_of[4], 1), 0, NBLK - 1).astype(jnp.int32)
    cell_lists = set_ends(jax.random.randint(streams_of[5], (DEVICES * NBLK, LC), 0, NCB + DEVICES * SLOTS), jax.random.fold_in(streams_of[5], 1), 0, (NCB + DEVICES * SLOTS) - 1).astype(jnp.int32)
    near_lists = set_ends(jax.random.randint(streams_of[6], (DEVICES * NBLK, LP), 0, NBLK + 4 * BPB), jax.random.fold_in(streams_of[6], 1), 0, (NBLK + 4 * BPB) - 1).astype(jnp.int32)
    return {"particles": particles, "tree_cells": tree_cells, "let_list": let_list, "let_count": let_count, "part_list": part_list, "cell_lists": cell_lists, "near_lists": near_lists}


SOFTENING = 0.0025
near_offsets = (1, -1, 2, -2)

def pair_forces(targets, cell_source, near_source):
    target_x = targets[0][:, None]
    target_y = targets[1][:, None]
    target_z = targets[2][:, None]
    delta_x = target_x - cell_source[0][None, :]
    delta_y = target_y - cell_source[1][None, :]
    delta_z = target_z - cell_source[2][None, :]
    inverse = 1.0 / jnp.sqrt(delta_x * delta_x + delta_y * delta_y + delta_z * delta_z + SOFTENING)
    inv_square = inverse * inverse
    inv_cube = inverse * inv_square
    inv_five = inv_cube * inv_square
    masses = cell_source[3][None, :]
    quad_x = cell_source[4][None, :] * delta_x + cell_source[7][None, :] * delta_y + cell_source[8][None, :] * delta_z
    quad_y = cell_source[7][None, :] * delta_x + cell_source[5][None, :] * delta_y + cell_source[9][None, :] * delta_z
    quad_z = cell_source[8][None, :] * delta_x + cell_source[9][None, :] * delta_y + cell_source[6][None, :] * delta_z
    contracted = delta_x * quad_x + delta_y * quad_y + delta_z * quad_z
    radial = -masses * inv_cube - 2.5 * contracted * inv_five * inv_square
    accel_x = lax.optimization_barrier(jnp.sum(radial * delta_x + quad_x * inv_five, axis=1))
    accel_y = lax.optimization_barrier(jnp.sum(radial * delta_y + quad_y * inv_five, axis=1))
    accel_z = lax.optimization_barrier(jnp.sum(radial * delta_z + quad_z * inv_five, axis=1))
    potential = lax.optimization_barrier(jnp.sum(-masses * inverse - 0.5 * contracted * inv_five, axis=1))
    near_x = target_x - near_source[0][None, :]
    near_y = target_y - near_source[1][None, :]
    near_z = target_z - near_source[2][None, :]
    near_inverse = 1.0 / jnp.sqrt(near_x * near_x + near_y * near_y + near_z * near_z + SOFTENING)
    near_masses = near_source[3][None, :]
    near_radial = -near_masses * near_inverse * near_inverse * near_inverse
    accel_x = accel_x + lax.optimization_barrier(jnp.sum(near_radial * near_x, axis=1))
    accel_y = accel_y + lax.optimization_barrier(jnp.sum(near_radial * near_y, axis=1))
    accel_z = accel_z + lax.optimization_barrier(jnp.sum(near_radial * near_z, axis=1))
    potential = potential + lax.optimization_barrier(jnp.sum(-near_masses * near_inverse, axis=1))
    return jnp.stack([accel_x, accel_y, accel_z, potential])

def block_forces(own_parts, cell_pool, near_pool, cell_ids, near_ids):

    def one_block(carried):
        targets, cell_row, near_row = carried
        cell_source = cell_pool[:, cell_row].reshape(10, -1)
        near_source = near_pool[:, near_row].reshape(4, -1)
        return pair_forces(targets, cell_source, near_source)
    result = lax.map(one_block, (jnp.moveaxis(own_parts, 1, 0), cell_ids, near_ids))
    return jnp.moveaxis(result, 0, 1).reshape(4, -1)

def reference(particles, tree_cells, let_list, let_count, part_list, cell_lists, near_lists):
    all_parts = particles.reshape(4, DEVICES, NBLK, BLK)
    all_cells = tree_cells.reshape(10, DEVICES, NCB, BLK)
    source_ids = jnp.arange(DEVICES, dtype=jnp.int32)
    slot_ids = jnp.arange(SLOTS, dtype=jnp.int32)
    cell_rows = cell_lists.reshape(DEVICES, NBLK, LC)
    near_rows = near_lists.reshape(DEVICES, NBLK, LP)

    def one_device(device):
        block_ids = let_list[:, device, :]
        received = all_cells[:, source_ids[:, None], block_ids]
        live_mask = slot_ids[None, :] < let_count[:, device][:, None]
        received = jnp.where(live_mask[None, :, :, None], received, jnp.float32(0.0))
        own_cells = all_cells[:, device]
        cell_pool = jnp.concatenate([own_cells, received.reshape(10, DEVICES * SLOTS, BLK)], axis=1)
        own_parts = all_parts[:, device]
        near_parts = [own_parts]
        for position, offset in enumerate(near_offsets):
            source = device - offset
            source_valid = (source >= 0) & (source < DEVICES)
            source_safe = jnp.clip(source, 0, DEVICES - 1).astype(jnp.int32)
            picked = all_parts[:, source_safe][:, part_list[source_safe, position]]
            near_parts.append(jnp.where(source_valid, picked, jnp.float32(0.0)))
        near_pool = jnp.concatenate(near_parts, axis=1)
        return block_forces(own_parts, cell_pool, near_pool, cell_rows[device], near_rows[device])
    result = lax.map(one_device, source_ids)
    return jnp.moveaxis(result, 0, 1).reshape(4, -1)
```

```python
import functools

import jax
import jax.numpy as jnp
from jax import lax
from jax.experimental import pallas as pl
from jax.experimental.pallas import tpu as pltpu
from jax.sharding import PartitionSpec as P

BLK = 128
ROWS = 16
KEEP = (0, 1, 2, 3, 4, 5, 7, 8, 9)

SOFTENING = 0.0025
near_offsets = (1, -1, 2, -2)
F32 = jnp.float32
B16 = jnp.bfloat16


def from_behind(block, axis, distance):
    devices = range(lax.axis_size(axis))
    route = [(i - distance, i) for i in devices if i - distance in devices]
    return lax.ppermute(block, axis, route)


def split3(value):
    high = value.astype(B16)
    rest = value - high.astype(F32)
    middle = rest.astype(B16)
    low = (rest - middle.astype(F32)).astype(B16)
    return high, middle, low


def split2(value):
    high = value.astype(B16)
    return high, (value - high.astype(F32)).astype(B16)


def stack_rows(rows):
    sub = lax.broadcasted_iota(jnp.int32, (8, BLK), 0)
    out = rows[0]
    for i in range(1, len(rows)):
        if rows[i] is not None:
            out = jnp.where(sub == i, rows[i], out)
    return out


def wide(row):
    return jnp.broadcast_to(row, (8, BLK))


def distance_rows(x, y, z):
    square = x * x + y * y + z * z + SOFTENING
    zero = jnp.zeros((8, BLK), F32)
    one = jnp.where(lax.broadcasted_iota(jnp.int32, (8, BLK), 0) == 2, 1.0, 0.0)
    return jnp.concatenate([stack_rows([x, y, z, square, zero, zero, zero, zero]), one], axis=0)


def quadrupole_rows(x, y, z, xx, yy, xy, xz, yz):
    xx, yy, xy, xz, yz = (2.5 * v for v in (xx, yy, xy, xz, yz))
    zz = -(xx + yy)
    qx = xx * x + xy * y + xz * z
    qy = xy * x + yy * y + yz * z
    qz = xz * x + yz * y + zz * z
    inner = qx * x + qy * y + qz * z
    zero = jnp.zeros((8, BLK), F32)
    first = stack_rows([qx, qy, qz, inner, xx, yy, zz, xy])
    second = stack_rows([xz, yz, zero, zero, zero, zero, zero, zero])
    return jnp.concatenate([first, second], axis=0)


def target_rows(x, y, z):
    one = jnp.ones((8, BLK), F32)
    zero = jnp.zeros((8, BLK), F32)
    first = stack_rows([-2 * x, -2 * y, -2 * z, one, x * x, y * y, z * z, 2 * x * y])
    second = stack_rows([2 * x * z, 2 * y * z, x * x + y * y + z * z, zero, zero, zero, zero, zero])
    return jnp.concatenate([first, second], axis=0)


def store_source(slot, weights, rows):
    high, middle, low = split3(rows)
    weights[slot, 0:ROWS] = high
    weights[slot, ROWS : 2 * ROWS] = middle
    weights[slot, 2 * ROWS :] = low


def six(weights):
    high, middle, low = weights[0:ROWS], weights[ROWS : 2 * ROWS], weights[2 * ROWS :]
    return jnp.concatenate([high, high, high, middle, middle, low], axis=0)


def contract(left, right):
    return lax.dot_general(left, right, (((1,), (1,)), ((), ())), preferred_element_type=F32)


def cell_pair(targets, weights, masses):
    both = jnp.dot(targets, six(weights), preferred_element_type=F32)
    inverse = lax.rsqrt(both[:, :BLK])
    square = inverse * inverse
    fifth = square * square * inverse
    pulled = masses * inverse
    radial = square * (pulled + both[:, BLK:] * fifth)
    left = jnp.concatenate([*split2(radial), *split2(fifth)], axis=1)
    near, quad = weights[:, :BLK], weights[:, BLK:]
    none = jnp.zeros_like(near)
    right = jnp.concatenate(
        [
            jnp.concatenate([near, near, none, none], axis=1),
            jnp.concatenate([none, none, quad, quad], axis=1),
        ],
        axis=0,
    )
    return contract(left, right), pulled


def near_pair(targets, first, second, masses):
    weights = jnp.concatenate([first, second], axis=1)
    both = jnp.dot(targets, six(weights), preferred_element_type=F32)
    inverse = lax.rsqrt(both)
    pulled = masses * inverse
    radial = pulled * (inverse * inverse)
    left = jnp.concatenate([*split2(radial[:, :BLK]), *split2(radial[:, BLK:])], axis=1)
    right = jnp.concatenate([first, first, second, second], axis=1)
    return contract(left, right), pulled[:, :BLK] + pulled[:, BLK:]


def tall(masses):
    return jnp.concatenate([masses] * (BLK // 8), axis=0)


def force_kernel(
    cell_lists, near_lists, particles, cells, moved, neighbours, out,
    targets, cell_weights, cell_masses, near_weights, near_masses,
):
    blocks = cell_lists.shape[0]
    own_cells = cells.shape[1] // BLK
    peers, _, slots, _ = moved.shape

    def put_cell(slot, x, y, z, mass, xx, yy, xy, xz, yz):
        store_source(
            slot,
            cell_weights,
            jnp.concatenate(
                [distance_rows(x, y, z), quadrupole_rows(x, y, z, xx, yy, xy, xz, yz)], axis=1
            ),
        )
        cell_masses[slot] = mass

    def put_near(slot, x, y, z, mass):
        store_source(slot, near_weights, distance_rows(x, y, z))
        near_masses[slot] = mass

    def own_step(b, unused):
        columns = pl.ds(pl.multiple_of(b * BLK, BLK), BLK)
        put_cell(b, *(wide(cells[f : f + 1, columns]) for f in KEEP))
        return unused

    lax.fori_loop(0, own_cells, own_step, 0, unroll=2)

    def moved_step(s, unused):
        for k in range(slots):
            put_cell(
                own_cells + s * slots + k,
                *(wide(moved[s, f, k : k + 1, :]) for f in range(len(KEEP))),
            )
        return unused

    lax.fori_loop(0, peers, moved_step, 0)

    def target_step(j, unused):
        columns = pl.ds(pl.multiple_of(j * BLK, BLK), BLK)
        x, y, z, mass = (wide(particles[f : f + 1, columns]) for f in range(4))
        put_near(j, x, y, z, mass)
        high, middle, low = (v.astype(F32) for v in split3(target_rows(x, y, z)))
        pad = jnp.zeros((BLK - 6 * ROWS, BLK), F32)
        rows = jnp.concatenate([high, middle, low, high, middle, high, pad], axis=0)
        targets[j] = jnp.transpose(rows).astype(B16)
        return unused

    lax.fori_loop(0, blocks, target_step, 0)

    def neighbour_step(b, unused):
        put_near(blocks + b, *(wide(neighbours[b, f : f + 1, :]) for f in range(4)))
        return unused

    lax.fori_loop(0, neighbours.shape[0], neighbour_step, 0)

    def block_step(j, unused):
        columns = pl.ds(pl.multiple_of(j * BLK, BLK), BLK)
        mine = targets[j][:, : 6 * ROWS]

        def cell_step(l, carried):
            total, potential = carried
            b = cell_lists[j, l]
            sums, pulled = cell_pair(mine, cell_weights[b], tall(cell_masses[b]))
            return total + sums, potential + pulled

        def near_step(l, carried):
            total, potential = carried
            b, c = near_lists[j, 2 * l], near_lists[j, 2 * l + 1]
            masses = jnp.concatenate([tall(near_masses[b]), tall(near_masses[c])], axis=1)
            sums, pulled = near_pair(mine, near_weights[b], near_weights[c], masses)
            return total + sums, potential + pulled

        total = jnp.zeros((BLK, 6 * ROWS), F32)
        potential = jnp.zeros((BLK, BLK), F32)
        total, potential = lax.fori_loop(0, cell_lists.shape[1], cell_step, (total, potential), unroll=4)
        near_total = jnp.zeros((BLK, 3 * ROWS), F32)
        near_total, potential = lax.fori_loop(
            0, near_lists.shape[1] // 2, near_step, (near_total, potential), unroll=4
        )
        pad = jnp.zeros((BLK, BLK - 6 * ROWS), F32)
        sums = jnp.transpose(jnp.concatenate([total, pad], axis=1))
        near_sums = jnp.transpose(
            jnp.concatenate([near_total, jnp.zeros((BLK, BLK - 3 * ROWS), F32)], axis=1)
        )
        pulls = jnp.sum(jnp.transpose(potential), axis=0, keepdims=True)
        finish(particles, columns, sums, near_sums, pulls, out)
        return unused

    lax.fori_loop(0, blocks, block_step, 0)


def finish(particles, columns, sums, near_sums, pulls, out):
    x, y, z = (particles[f : f + 1, columns] for f in range(3))
    near = sums[0:16] + sums[16:32] + sums[32:48]
    near = near + near_sums[0:16] + near_sums[16:32] + near_sums[32:48]
    quad = sums[48:64] + sums[64:80] + sums[80:96]

    def row(values, i):
        return values[i : i + 1]

    whole = row(near, 10)
    qx, qy, qz, inner, xx, yy, zz, xy, xz, yz = (row(quad, i) for i in range(10))
    ax = xx * x + xy * y + xz * z
    ay = xy * x + yy * y + yz * z
    az = xz * x + yz * y + zz * z
    out[0:1, columns] = 0.4 * (ax - qx) - (x * whole - row(near, 0))
    out[1:2, columns] = 0.4 * (ay - qy) - (y * whole - row(near, 1))
    out[2:3, columns] = 0.4 * (az - qz) - (z * whole - row(near, 2))
    bent = ax * x + ay * y + az * z - 2 * (qx * x + qy * y + qz * z) + inner
    out[3:4, columns] = -pulls - 0.2 * bent


def exchange_cells(chosen):
    return lax.all_to_all(chosen, ("gx", "gy"), split_axis=0, concat_axis=0, tiled=True)


def body(particles, tree_cells, let_list, let_count, part_list, cell_lists, near_lists):
    part_blocks = jnp.transpose(particles.reshape(4, -1, BLK), (1, 0, 2))
    kept = jnp.concatenate([tree_cells[:6], tree_cells[7:]], axis=0)
    cell_blocks = jnp.transpose(kept.reshape(len(KEEP), -1, BLK), (1, 0, 2))
    peers = lax.axis_size(("gx", "gy"))
    slots = let_list.shape[2]
    live = lax.broadcasted_iota(jnp.int32, (peers, slots), 1) < let_count[0][:, None]
    chosen = jnp.where(live[:, :, None, None], cell_blocks[let_list[0]], 0.0)
    moved = exchange_cells(jnp.transpose(chosen, (0, 2, 1, 3)))
    near_parts = []
    for position, offset in enumerate(near_offsets):
        picked = part_blocks[part_list[0, position]]
        near_parts.append(from_behind(picked, ("gx", "gy"), offset))
    neighbours = jnp.concatenate(near_parts, axis=0)

    blocks = cell_lists.shape[0]
    pool = tree_cells.shape[1] // BLK + peers * slots
    near_pool = blocks + neighbours.shape[0]
    smem = pl.BlockSpec(memory_space=pltpu.SMEM)
    vmem = pl.BlockSpec(memory_space=pltpu.VMEM)
    return pl.pallas_call(
        force_kernel,
        out_shape=jax.ShapeDtypeStruct(particles.shape, F32),
        in_specs=[smem, smem, vmem, vmem, vmem, vmem],
        out_specs=vmem,
        scratch_shapes=[
            pltpu.VMEM((blocks, BLK, BLK), B16),
            pltpu.VMEM((pool, 3 * ROWS, 2 * BLK), B16),
            pltpu.VMEM((pool, 8, BLK), F32),
            pltpu.VMEM((near_pool, 3 * ROWS, BLK), B16),
            pltpu.VMEM((near_pool, 8, BLK), F32),
        ],
        compiler_params=pltpu.CompilerParams(vmem_limit_bytes=48 * 2**20),
    )(cell_lists, near_lists, particles, tree_cells, moved, neighbours)


def solution(mesh):
    return jax.shard_map(
        body,
        mesh=mesh,
        in_specs=(
            P(None, ("gx", "gy")),
            P(None, ("gx", "gy")),
            P(("gx", "gy"), None, None),
            P(("gx", "gy"), None),
            P(("gx", "gy"), None, None),
            P(("gx", "gy"), None),
            P(("gx", "gy"), None),
        ),
        out_specs=P(None, ("gx", "gy")),
        check_vma=False,
    )
```

```python
import functools

import jax
import jax.numpy as jnp
from jax import lax
from jax.experimental import pallas as pl
from jax.experimental.pallas import tpu as pltpu
from jax.sharding import PartitionSpec as P

BLK = 128
ROWS = 16
SUMS = 4
SOFTENING = 0.0025
near_offsets = (1, -1, 2, -2)
F32 = jnp.float32
B16 = jnp.bfloat16


def from_behind(block, axis, distance):
    devices = range(lax.axis_size(axis))
    route = [(i - distance, i) for i in devices if i - distance in devices]
    return lax.ppermute(block, axis, route)


def at_block(index):
    return pl.ds(pl.multiple_of(index * BLK, BLK), BLK)


def split3(value):
    high = value.astype(B16)
    rest = value - high.astype(F32)
    middle = rest.astype(B16)
    low = (rest - middle.astype(F32)).astype(B16)
    return high, middle, low


def split2(value):
    high = value.astype(B16)
    return high, (value - high.astype(F32)).astype(B16)


def stack_rows(rows):
    sub = lax.broadcasted_iota(jnp.int32, (8, BLK), 0)
    out = rows[0]
    for i in range(1, len(rows)):
        out = jnp.where(sub == i, rows[i], out)
    return out


def wide(row):
    return jnp.broadcast_to(row, (8, BLK))


def quadrupole_rows(x, y, z, xx, yy, xy, xz, yz):
    xx, yy, xy, xz, yz = (2.5 * v for v in (xx, yy, xy, xz, yz))
    zz = -(xx + yy)
    qx = xx * x + xy * y + xz * z
    qy = xy * x + yy * y + yz * z
    qz = xz * x + yz * y + zz * z
    inner = qx * x + qy * y + qz * z
    first = stack_rows([qx, qy, qz, inner, xx, yy, zz, xy])
    second = stack_rows([jnp.zeros((8, BLK), F32), yz, xz])
    return jnp.concatenate([first, second], axis=0)


def target_rows(x, y, z):
    one = jnp.ones((8, BLK), F32)
    first = stack_rows([-2 * x, -2 * y, -2 * z, one, x * x, y * y, z * z, 2 * x * y])
    second = stack_rows([jnp.zeros((8, BLK), F32), 2 * y * z, 2 * x * z])
    return jnp.concatenate([first, second], axis=0)


def put_weights(weights, slot, rows):
    high, middle, low = split3(rows)
    weights[slot, 0:ROWS] = high
    weights[slot, ROWS : 2 * ROWS] = middle
    weights[slot, 2 * ROWS :] = low


def six(weights):
    high, middle, low = weights[0:ROWS], weights[ROWS : 2 * ROWS], weights[2 * ROWS :]
    return jnp.concatenate([high, high, high, middle, middle, low], axis=0)


def contract(left, right):
    return lax.dot_general(left, right, (((1,), (1,)), ((), ())), preferred_element_type=F32)


def pick_kernel(let_list, let_count, part_list, cells, particles, chosen, *picked):
    peers, slots = let_list.shape
    sub = lax.broadcasted_iota(jnp.int32, (4, BLK), 0)

    def peer_step(d, unused):
        count = let_count[0, d]
        for k in range(slots):
            columns = at_block(let_list[d, k])
            live = k < count
            chosen[d, k] = jnp.where(live, cells[0:4, columns], 0.0)
            quad = jnp.where(sub == 2, cells[8:9, columns], cells[4:8, columns])
            chosen[d, slots + k] = jnp.where(live, quad, 0.0)
            chosen[d, 2 * slots, k : k + 1, :] = jnp.where(live, cells[9:10, columns], 0.0)
        return unused

    lax.fori_loop(0, peers, peer_step, 0, unroll=2)
    for position, out in enumerate(picked):
        for k in range(part_list.shape[1]):
            out[k] = particles[:, at_block(part_list[position, k])]


def cell_group(size, j, first, lists, targets, spread, places, weights, sums, quads):
    blocks = [lists[j, first + i] for i in range(size)]
    coefficients = jnp.concatenate([six(weights[b]) for b in blocks], axis=1)
    bent = jnp.dot(targets[j], coefficients, preferred_element_type=F32)
    left = []
    for low in range(0, BLK, 16):
        rows = slice(low, low + 16)
        x, y, z = (spread[j, f, rows] for f in range(3))
        ax, ay, az, potential = (sums[j, f, rows] for f in range(SUMS))
        parts = []
        for i, b in enumerate(blocks):
            rx, ry, rz = x - places[b, 0:1, :], y - places[b, 1:2, :], z - places[b, 2:3, :]
            inverse = lax.rsqrt(rx * rx + ry * ry + (rz * rz + SOFTENING))
            square = inverse * inverse
            fifth = square * square * inverse
            pulled = inverse * places[b, 3:4, :]
            radial = square * (pulled + bent[rows, i * BLK : (i + 1) * BLK] * fifth)
            ax += radial * rx
            ay += radial * ry
            az += radial * rz
            potential += pulled
            parts += split2(fifth)
        for f, value in enumerate((ax, ay, az, potential)):
            sums[j, f, rows] = value
        left.append(jnp.concatenate(parts, axis=1))
    right = jnp.concatenate([weights[b] for b in blocks for _ in range(2)], axis=1)
    quads[j, :, : 3 * ROWS] += contract(jnp.concatenate(left, axis=0), right)


def near_group(size, j, first, lists, spread, places, sums):
    blocks = [lists[j, first + i] for i in range(size)]
    for low in range(0, BLK, 16):
        rows = slice(low, low + 16)
        x, y, z = (spread[j, f, rows] for f in range(3))
        ax, ay, az, potential = (sums[j, f, rows] for f in range(SUMS))
        for b in blocks:
            rx, ry, rz = x - places[b, 0:1, :], y - places[b, 1:2, :], z - places[b, 2:3, :]
            inverse = lax.rsqrt(rx * rx + ry * ry + (rz * rz + SOFTENING))
            pulled = inverse * places[b, 3:4, :]
            radial = pulled * (inverse * inverse)
            ax += radial * rx
            ay += radial * ry
            az += radial * rz
            potential += pulled
        for f, value in enumerate((ax, ay, az, potential)):
            sums[j, f, rows] = value


def in_groups(count, group):
    fours = (count + 1) // 4

    def four(i, unused):
        group(4, 4 * i)
        return unused

    lax.fori_loop(0, fours, four, 0)

    @pl.when(4 * fours < count)
    def _():
        group(2, 4 * fours)


def keep_some(j, source, target, wanted, nothing):
    count = jnp.int32(0)
    for l in range(source.shape[1]):
        slot, live = wanted(source[j, l])
        target[j, count] = slot
        count = count + live.astype(jnp.int32)
    for extra in range(3):
        target[j, count + extra] = nothing
    return count


def spread_targets(j, columns, spread):
    for f in range(3):
        spread[j, f] = jnp.broadcast_to(columns[j, :, f : f + 1], (BLK, BLK)) * (-0.5)


def clear(j, sums, quads):
    for f in range(SUMS):
        sums[j, f] = jnp.zeros((BLK, BLK), F32)
    quads[j] = jnp.zeros((BLK, BLK), F32)


def forces_of(j, particles, sums, quads):
    lane = lax.broadcasted_iota(jnp.int32, (BLK, BLK), 1)
    mixed = quads[j]
    for f in range(SUMS):
        mixed = jnp.where(lane == 64 + f, jnp.sum(sums[j, f], axis=1, keepdims=True), mixed)
    mixed = jnp.transpose(mixed)
    quad = mixed[0:16] + mixed[16:32] + mixed[32:48]
    qx, qy, qz, inner, xx, yy, zz, xy = (quad[i : i + 1] for i in range(8))
    yz, xz = quad[9:10], quad[10:11]
    sx, sy, sz, pulls = (mixed[64 + f : 65 + f] for f in range(SUMS))
    x, y, z = (particles[f : f + 1, at_block(j)] for f in range(3))
    ax = xx * x + xy * y + xz * z
    ay = xy * x + yy * y + yz * z
    az = xz * x + yz * y + zz * z
    bent = ax * x + ay * y + az * z - 2 * (qx * x + qy * y + qz * z) + inner
    return (
        0.4 * (ax - qx) - sx,
        0.4 * (ay - qy) - sy,
        0.4 * (az - qz) - sz,
        -pulls - 0.2 * bent,
    )


def own_kernel(
    cell_lists, near_lists, particles, cells, out, targets, columns,
    lists, near_kept, spread, places, weights, near_places, sums, quads,
):
    blocks = cell_lists.shape[0]
    own_cells = cells.shape[1] // BLK

    def prepare_cell(b, unused):
        x, y, z, _, xx, yy, _, xy, xz, yz = (wide(cells[f : f + 1, at_block(b)]) for f in range(10))
        put_weights(weights, b, quadrupole_rows(x, y, z, xx, yy, xy, xz, yz))
        places[b, 0:4, :] = cells[0:4, at_block(b)]
        return unused

    lax.fori_loop(0, own_cells, prepare_cell, 0, unroll=4)
    weights[own_cells] = jnp.zeros((3 * ROWS, BLK), B16)
    places[own_cells] = jnp.zeros((8, BLK), F32)
    near_places[blocks] = jnp.zeros((8, BLK), F32)

    def prepare_target(j, unused):
        near_places[j, 0:4, :] = particles[:, at_block(j)]
        x, y, z = (wide(particles[f : f + 1, at_block(j)]) for f in range(3))
        high, middle, low = (v.astype(F32) for v in split3(target_rows(x, y, z)))
        exact = target_rows(x, y, z)
        pad = jnp.zeros((BLK - 7 * ROWS, BLK), F32)
        rows = jnp.concatenate([high, middle, low, high, middle, high, exact, pad], axis=0)
        turned = jnp.transpose(rows)
        targets[j] = turned[:, : 6 * ROWS].astype(B16)
        columns[j] = turned[:, 6 * ROWS : 7 * ROWS]
        spread_targets(j, columns, spread)
        clear(j, sums, quads)
        return unused

    lax.fori_loop(0, blocks, prepare_target, 0)

    def block_step(j, unused):
        count = keep_some(j, cell_lists, lists, lambda b: (b, b < own_cells), own_cells)
        near_count = keep_some(j, near_lists, near_kept, lambda b: (b, b < blocks), blocks)
        in_groups(
            count,
            lambda size, first: cell_group(
                size, j, first, lists, targets, spread, places, weights, sums, quads
            ),
        )
        in_groups(
            near_count,
            lambda size, first: near_group(size, j, first, near_kept, spread, near_places, sums),
        )
        return unused

    lax.fori_loop(0, blocks, block_step, 0)

    def finish_step(j, unused):
        for f, row in enumerate(forces_of(j, particles, sums, quads)):
            out[f : f + 1, at_block(j)] = row
        return unused

    lax.fori_loop(0, blocks, finish_step, 0, unroll=2)


def moved_kernel(
    own_cells, cell_lists, near_lists, particles, targets, columns, partial, moved, *rest
):
    neighbours, (out, counts, lists, near_kept, spread, places, weights, near_places, sums, quads) = (
        rest[:-10], rest[-10:],
    )
    blocks = cell_lists.shape[0]
    peers, slots = moved.shape[0], moved.shape[2]
    near_moved = len(neighbours) * neighbours[0].shape[0]

    def prepare_peer(s, unused):
        alive = jnp.zeros((4, BLK), jnp.int32)
        for k in range(slots):
            b = s * slots + k
            x, y, z = (wide(moved[s, k, f : f + 1, :]) for f in range(3))
            xx, yy, xz, xy = (wide(moved[s, slots + k, f : f + 1, :]) for f in range(4))
            yz = wide(moved[s, 2 * slots, k : k + 1, :])
            put_weights(weights, b, quadrupole_rows(x, y, z, xx, yy, xy, xz, yz))
            places[b, 0:4, :] = moved[s, k]
            some = jnp.abs(moved[s, k]) + jnp.abs(moved[s, slots + k])
            some = some + jnp.abs(moved[s, 2 * slots, k : k + 1, :])
            alive = jnp.where(some > 0, k + 1, alive)
        counts[s] = jnp.max(alive)
        return unused

    lax.fori_loop(0, peers, prepare_peer, 0)
    weights[peers * slots] = jnp.zeros((3 * ROWS, BLK), B16)
    places[peers * slots] = jnp.zeros((8, BLK), F32)
    for i, block in enumerate(neighbours):
        for k in range(block.shape[0]):
            near_places[i * block.shape[0] + k, 0:4, :] = block[k]
    near_places[near_moved] = jnp.zeros((8, BLK), F32)

    def prepare_target(j, unused):
        spread_targets(j, columns, spread)
        clear(j, sums, quads)
        return unused

    lax.fori_loop(0, blocks, prepare_target, 0)

    def wanted(b):
        slot = jnp.maximum(b - own_cells, 0)
        live = (b >= own_cells) & (slot % slots < counts[slot // slots])
        return slot, live

    def block_step(j, unused):
        count = keep_some(j, cell_lists, lists, wanted, peers * slots)
        near_count = keep_some(
            j, near_lists, near_kept, lambda b: (b - blocks, b >= blocks), near_moved
        )
        in_groups(
            count,
            lambda size, first: cell_group(
                size, j, first, lists, targets, spread, places, weights, sums, quads
            ),
        )
        in_groups(
            near_count,
            lambda size, first: near_group(size, j, first, near_kept, spread, near_places, sums),
        )
        return unused

    lax.fori_loop(0, blocks, block_step, 0)

    def finish_step(j, unused):
        for f, row in enumerate(forces_of(j, particles, sums, quads)):
            out[f : f + 1, at_block(j)] = row + partial[f : f + 1, at_block(j)]
        return unused

    lax.fori_loop(0, blocks, finish_step, 0, unroll=2)


def scratch(blocks, cells, near, list_width, near_width):
    return [
        pltpu.SMEM((blocks, list_width + 4), jnp.int32),
        pltpu.SMEM((blocks, near_width + 4), jnp.int32),
        pltpu.VMEM((blocks, 3, BLK, BLK), F32),
        pltpu.VMEM((cells + 1, 8, BLK), F32),
        pltpu.VMEM((cells + 1, 3 * ROWS, BLK), B16),
        pltpu.VMEM((near + 1, 8, BLK), F32),
        pltpu.VMEM((blocks, SUMS, BLK, BLK), F32),
        pltpu.VMEM((blocks, BLK, BLK), F32),
    ]


def body(particles, tree_cells, let_list, let_count, part_list, cell_lists, near_lists):
    peers = lax.axis_size(("gx", "gy"))
    slots = let_list.shape[2]
    near_slots = part_list.shape[2]
    blocks, list_width = cell_lists.shape
    near_width = near_lists.shape[1]
    own_cells = tree_cells.shape[1] // BLK
    smem = pl.BlockSpec(memory_space=pltpu.SMEM)
    vmem = pl.BlockSpec(memory_space=pltpu.VMEM)
    params = pltpu.CompilerParams(vmem_limit_bytes=48 * 2**20)

    chosen, *picked = pl.pallas_call(
        pick_kernel,
        out_shape=[jax.ShapeDtypeStruct((peers, 2 * slots + 1, 4, BLK), F32)]
        + [jax.ShapeDtypeStruct((near_slots, 4, BLK), F32) for _ in near_offsets],
        in_specs=[smem, smem, smem, vmem, vmem],
        out_specs=[vmem] * (1 + len(near_offsets)),
        compiler_params=params,
    )(let_list[0], let_count, part_list[0], tree_cells, particles)
    moved = lax.all_to_all(chosen, ("gx", "gy"), split_axis=0, concat_axis=0, tiled=True)
    neighbours = [
        from_behind(block, ("gx", "gy"), offset) for block, offset in zip(picked, near_offsets)
    ]

    partial, targets, columns = pl.pallas_call(
        own_kernel,
        out_shape=[
            jax.ShapeDtypeStruct(particles.shape, F32),
            jax.ShapeDtypeStruct((blocks, BLK, 6 * ROWS), B16),
            jax.ShapeDtypeStruct((blocks, BLK, ROWS), F32),
        ],
        in_specs=[smem, smem, vmem, vmem],
        out_specs=[vmem] * 3,
        scratch_shapes=scratch(blocks, own_cells, blocks, list_width, near_width),
        compiler_params=params,
        cost_estimate=pl.CostEstimate(flops=10**9, bytes_accessed=10**6, transcendentals=10**6),
    )(cell_lists, near_lists, particles, tree_cells)

    near_moved = len(neighbours) * near_slots
    return pl.pallas_call(
        functools.partial(moved_kernel, own_cells),
        out_shape=jax.ShapeDtypeStruct(particles.shape, F32),
        in_specs=[smem, smem] + [vmem] * (5 + len(neighbours)),
        out_specs=vmem,
        scratch_shapes=[pltpu.SMEM((peers,), jnp.int32)]
        + scratch(blocks, peers * slots, near_moved, list_width, near_width),
        compiler_params=params,
    )(cell_lists, near_lists, particles, targets, columns, partial, moved, *neighbours)


def solution(mesh):
    return jax.shard_map(
        body,
        mesh=mesh,
        in_specs=(
            P(None, ("gx", "gy")),
            P(None, ("gx", "gy")),
            P(("gx", "gy"), None, None),
            P(("gx", "gy"), None),
            P(("gx", "gy"), None, None),
            P(("gx", "gy"), None),
            P(("gx", "gy"), None),
        ),
        out_specs=P(None, ("gx", "gy")),
        check_vma=False,
    )
```

```python
import functools

import jax
import jax.numpy as jnp
from jax import lax
from jax.experimental import pallas as pl
from jax.experimental.pallas import tpu as pltpu
from jax.sharding import PartitionSpec as P

BLK = 128
ROWS = 16
SUMS = 4
SOFTENING = 0.0025
near_offsets = (1, -1, 2, -2)
F32 = jnp.float32
B16 = jnp.bfloat16


def at_block(index):
    return pl.ds(pl.multiple_of(index * BLK, BLK), BLK)


def split3(value):
    high = value.astype(B16)
    rest = value - high.astype(F32)
    middle = rest.astype(B16)
    low = (rest - middle.astype(F32)).astype(B16)
    return high, middle, low


def split2(value):
    high = value.astype(B16)
    return high, (value - high.astype(F32)).astype(B16)


def stack_rows(rows):
    sub = lax.broadcasted_iota(jnp.int32, (8, BLK), 0)
    out = rows[0]
    for i in range(1, len(rows)):
        out = jnp.where(sub == i, rows[i], out)
    return out


def wide(row):
    return jnp.broadcast_to(row, (8, BLK))


def quadrupole_rows(x, y, z, xx, yy, xy, xz, yz):
    xx, yy, xy, xz, yz = (2.5 * v for v in (xx, yy, xy, xz, yz))
    zz = -(xx + yy)
    qx = xx * x + xy * y + xz * z
    qy = xy * x + yy * y + yz * z
    qz = xz * x + yz * y + zz * z
    inner = qx * x + qy * y + qz * z
    return [qx, qy, qz, inner, xx, yy, zz, xy, yz, xz]


def target_rows(x, y, z):
    one = jnp.ones((8, BLK), F32)
    first = stack_rows([-2 * x, -2 * y, -2 * z, one, x * x, y * y, z * z, 2 * x * y])
    second = stack_rows([2 * y * z, 2 * x * z] + [jnp.zeros((8, BLK), F32)] * 6)
    return jnp.concatenate([first, second], axis=0)


def six(weights):
    high, middle, low = weights[0:ROWS], weights[ROWS : 2 * ROWS], weights[2 * ROWS :]
    return jnp.concatenate([high, high, high, middle, middle, low], axis=0)


def contract(left, right):
    return lax.dot_general(left, right, (((1,), (1,)), ((), ())), preferred_element_type=F32)


def pick_kernel(let_list, let_count, part_list, cells, particles, chosen):
    slots, peers = let_list.shape
    sub = lax.broadcasted_iota(jnp.int32, (4, BLK), 0)

    def peer_step(d, unused):
        count = let_count[0, d]
        for k in range(slots):
            columns = at_block(let_list[k, d])
            live = k < count
            chosen[d, k] = jnp.where(live, cells[0:4, columns], 0.0)
            quad = jnp.where(sub == 2, cells[8:9, columns], cells[4:8, columns])
            chosen[d, slots + k] = jnp.where(live, quad, 0.0)
            chosen[d, 2 * slots, k : k + 1, :] = jnp.where(live, cells[9:10, columns], 0.0)
        return unused

    lax.fori_loop(0, peers, peer_step, 0, unroll=4)
    for position, offset in enumerate(near_offsets):
        d = lax.axis_index(("gx", "gy")) + offset

        @pl.when((d >= 0) & (d < peers))
        def _():
            for k in range(part_list.shape[1]):
                chosen[d, 2 * slots + 1 + k] = particles[:, at_block(part_list[position, k])]


def put_eight(first, fields, rows):
    for i, value in enumerate(fields):
        rows[pl.ds(first * ROWS + i, 8, stride=ROWS), :] = value
    for i in range(len(fields), ROWS):
        rows[pl.ds(first * ROWS + i, 8, stride=ROWS), :] = jnp.zeros((8, BLK), F32)


def put_weights(count, rows, weights):
    def step(b, unused):
        high, middle, low = split3(rows[pl.ds(pl.multiple_of(b * ROWS, ROWS), ROWS), :])
        weights[b, 0:ROWS] = high
        weights[b, ROWS : 2 * ROWS] = middle
        weights[b, 2 * ROWS :] = low
        return unused

    lax.fori_loop(0, count, step, 0, unroll=8)


def cell_group(size, j, first, lists, targets, spread, places, weights, sums, quads):
    blocks = [lists[j, first + i] for i in range(size)]
    coefficients = jnp.concatenate([six(weights[b]) for b in blocks], axis=1)
    bent = jnp.dot(targets[j], coefficients, preferred_element_type=F32)
    left = []
    for low in range(0, BLK, 16):
        rows = slice(low, low + 16)
        x, y, z = (spread[j, f, rows] for f in range(3))
        ax, ay, az, potential = (sums[j, f, rows] for f in range(SUMS))
        parts = []
        for i, b in enumerate(blocks):
            rx, ry, rz = x - places[b, 0:1, :], y - places[b, 1:2, :], z - places[b, 2:3, :]
            inverse = lax.rsqrt(rx * rx + ry * ry + (rz * rz + SOFTENING))
            square = inverse * inverse
            fifth = square * square * inverse
            pulled = inverse * places[b, 3:4, :]
            radial = square * (pulled + bent[rows, i * BLK : (i + 1) * BLK] * fifth)
            ax += radial * rx
            ay += radial * ry
            az += radial * rz
            potential += pulled
            parts += split2(fifth)
        for f, value in enumerate((ax, ay, az, potential)):
            sums[j, f, rows] = value
        left.append(jnp.concatenate(parts, axis=1))
    right = jnp.concatenate([weights[b] for b in blocks for _ in range(2)], axis=1)
    quads[j, :, : 3 * ROWS] += contract(jnp.concatenate(left, axis=0), right)


def near_group(size, j, first, lists, spread, places, sums):
    blocks = [lists[j, first + i] for i in range(size)]
    for low in range(0, BLK, 16):
        rows = slice(low, low + 16)
        x, y, z = (spread[j, f, rows] for f in range(3))
        ax, ay, az, potential = (sums[j, f, rows] for f in range(SUMS))
        for b in blocks:
            rx, ry, rz = x - places[b, 0:1, :], y - places[b, 1:2, :], z - places[b, 2:3, :]
            inverse = lax.rsqrt(rx * rx + ry * ry + (rz * rz + SOFTENING))
            pulled = inverse * places[b, 3:4, :]
            radial = pulled * (inverse * inverse)
            ax += radial * rx
            ay += radial * ry
            az += radial * rz
            potential += pulled
        for f, value in enumerate((ax, ay, az, potential)):
            sums[j, f, rows] = value


def in_groups(count, group):
    fours = (count + 1) // 4

    def four(i, unused):
        group(4, 4 * i)
        return unused

    lax.fori_loop(0, fours, four, 0)

    @pl.when(4 * fours < count)
    def _():
        group(2, 4 * fours)


def keep_some(j, source, width, base, target, counts, live, nothing):
    count = jnp.int32(0)
    for l in range(width):
        index = source(j, l)
        target[j, count] = index - base
        count = count + live(index)
    for extra in range(3):
        target[j, count + extra] = nothing
    counts[j] = count


def forces_of(j, particles, sums, quads):
    lane = lax.broadcasted_iota(jnp.int32, (BLK, BLK), 1)
    mixed = quads[j]
    for f in range(SUMS):
        mixed = jnp.where(lane == 64 + f, jnp.sum(sums[j, f], axis=1, keepdims=True), mixed)
    mixed = jnp.transpose(mixed)
    quad = mixed[0:16] + mixed[16:32] + mixed[32:48]
    qx, qy, qz, inner, xx, yy, zz, xy = (quad[i : i + 1] for i in range(8))
    yz, xz = quad[8:9], quad[9:10]
    sx, sy, sz, pulls = (mixed[64 + f : 65 + f] for f in range(SUMS))
    x, y, z = (particles[f : f + 1, at_block(j)] for f in range(3))
    ax = xx * x + xy * y + xz * z
    ay = xy * x + yy * y + yz * z
    az = xz * x + yz * y + zz * z
    bent = ax * x + ay * y + az * z - 2 * (qx * x + qy * y + qz * z) + inner
    return (
        0.4 * (ax - qx) - sx,
        0.4 * (ay - qy) - sy,
        0.4 * (az - qz) - sz,
        -pulls - 0.2 * bent,
    )


def own_kernel(
    cell_lists, near_lists, particles, cells, targets, spread, sums, quads,
    lists, list_counts, near_kept, near_counts, places, weights, near_places, fields, rows,
):
    blocks = cell_lists.shape[0]
    own_cells = cells.shape[1] // BLK

    def by_field(b, unused):
        fields[pl.ds(b, 8, stride=own_cells), :] = cells[0:8, at_block(b)]
        fields[pl.ds(8 * own_cells + b, 2, stride=own_cells), :] = cells[8:10, at_block(b)]
        places[b] = cells[0:8, at_block(b)]
        return unused

    lax.fori_loop(0, own_cells, by_field, 0, unroll=8)

    def eight(g, unused):
        first = pl.multiple_of(8 * g, 8)
        x, y, z, _, xx, yy, _, xy, xz, yz = (
            fields[pl.ds(f * own_cells + first, 8), :] for f in range(10)
        )
        put_eight(first, quadrupole_rows(x, y, z, xx, yy, xy, xz, yz), rows)
        return unused

    lax.fori_loop(0, own_cells // 8, eight, 0, unroll=2)
    put_weights(own_cells, rows, weights)
    weights[own_cells] = jnp.zeros((3 * ROWS, BLK), B16)
    places[own_cells] = jnp.zeros((8, BLK), F32)
    near_places[blocks] = jnp.zeros((8, BLK), F32)

    def prepare_target(j, unused):
        near_places[j, 0:4, :] = particles[:, at_block(j)]
        x, y, z = (wide(particles[f : f + 1, at_block(j)]) for f in range(3))
        exact = target_rows(x, y, z)
        high, middle, low = (v.astype(F32) for v in split3(exact))
        pad = jnp.zeros((BLK - 7 * ROWS, BLK), F32)
        turned = jnp.transpose(
            jnp.concatenate([high, middle, low, high, middle, high, exact, pad], axis=0)
        )
        targets[j] = turned[:, : 6 * ROWS].astype(B16)
        for f in range(3):
            column = turned[:, 6 * ROWS + f : 6 * ROWS + f + 1]
            spread[j, f] = jnp.broadcast_to(column, (BLK, BLK)) * (-0.5)
        for f in range(SUMS):
            sums[j, f] = jnp.zeros((BLK, BLK), F32)
        quads[j] = jnp.zeros((BLK, BLK), F32)
        keep_some(
            j, lambda j, l: cell_lists[j, l], cell_lists.shape[1], 0, lists, list_counts,
            lambda b: (b < own_cells).astype(jnp.int32), own_cells,
        )
        keep_some(
            j, lambda j, l: near_lists[l, j], near_lists.shape[0], 0, near_kept, near_counts,
            lambda b: (b < blocks).astype(jnp.int32), blocks,
        )
        return unused

    lax.fori_loop(0, blocks, prepare_target, 0, unroll=2)
    add_all(
        blocks, lists, list_counts, near_kept, near_counts, targets, spread, places, weights,
        near_places, sums, quads,
    )


def add_all(
    blocks, lists, list_counts, near_kept, near_counts, targets, spread, places, weights,
    near_places, sums, quads,
):
    def block_step(j, unused):
        in_groups(
            list_counts[j],
            lambda size, first: cell_group(
                size, j, first, lists, targets, spread, places, weights, sums, quads
            ),
        )
        in_groups(
            near_counts[j],
            lambda size, first: near_group(size, j, first, near_kept, spread, near_places, sums),
        )
        return unused

    lax.fori_loop(0, blocks, block_step, 0)


def moved_kernel(
    own_cells, near_slots, cell_lists, near_lists, particles, targets, spread, own_sums, own_quads,
    moved, out,
    lists, list_counts, near_kept, near_counts, places, weights, near_places, fields, rows,
    sums, quads, live,
):
    blocks = cell_lists.shape[0]
    peers, slots = moved.shape[0], moved.shape[2]
    count = peers * slots
    near_moved = len(near_offsets) * near_slots
    me = lax.axis_index(("gx", "gy"))

    def by_field(s, unused):
        for k in range(slots):
            b = s * slots + k
            fields[pl.ds(b, 4, stride=count), :] = moved[s, k]
            fields[pl.ds(4 * count + b, 4, stride=count), :] = moved[s, slots + k]
            places[b, 0:4, :] = moved[s, k]
        fields[pl.ds(8 * count + s * slots, slots), :] = moved[s, 2 * slots]
        return unused

    lax.fori_loop(0, peers, by_field, 0, unroll=2)

    def none_live(b, unused):
        live[b] = 0
        return unused

    lax.fori_loop(0, own_cells, none_live, 0, unroll=8)
    bit = lax.broadcasted_iota(jnp.int32, (8, BLK), 0)

    def eight(g, unused):
        first = pl.multiple_of(8 * g, 8)
        x, y, z, mass, xx, yy, xz, xy, yz = (
            fields[pl.ds(f * count + first, 8), :] for f in range(9)
        )
        put_eight(first, quadrupole_rows(x, y, z, xx, yy, xy, xz, yz), rows)
        some = (mass != 0) | (xx != 0) | (yy != 0) | (xy != 0) | (xz != 0) | (yz != 0)
        some = jnp.max(jnp.where(some, 1.0, 0.0), axis=1, keepdims=True)
        code = jnp.sum(some * jnp.left_shift(1, bit[:, 0:1]).astype(F32)).astype(jnp.int32)
        for i in range(8):
            live[own_cells + first + i] = jnp.right_shift(code, i) & 1
        return unused

    lax.fori_loop(0, count // 8, eight, 0, unroll=4)
    put_weights(count, rows, weights)
    weights[count] = jnp.zeros((3 * ROWS, BLK), B16)
    places[count] = jnp.zeros((8, BLK), F32)
    for position, offset in enumerate(near_offsets):
        source = me - offset
        there = (source >= 0) & (source < peers)
        safe = jnp.clip(source, 0, peers - 1)
        for k in range(near_slots):
            block = moved[safe, 2 * slots + 1 + k]
            near_places[position * near_slots + k, 0:4, :] = jnp.where(there, block, 0.0)
    near_places[near_moved] = jnp.zeros((8, BLK), F32)

    def prepare_target(j, unused):
        sums[j] = own_sums[j]
        quads[j] = own_quads[j]
        keep_some(
            j, lambda j, l: cell_lists[j, l], cell_lists.shape[1], own_cells, lists, list_counts,
            lambda b: live[b], count,
        )
        keep_some(
            j, lambda j, l: near_lists[l, j], near_lists.shape[0], blocks, near_kept, near_counts,
            lambda b: (b >= blocks).astype(jnp.int32), near_moved,
        )
        return unused

    lax.fori_loop(0, blocks, prepare_target, 0, unroll=2)
    add_all(
        blocks, lists, list_counts, near_kept, near_counts, targets, spread, places, weights,
        near_places, sums, quads,
    )

    def finish_step(j, unused):
        for f, row in enumerate(forces_of(j, particles, sums, quads)):
            out[f : f + 1, at_block(j)] = row
        return unused

    lax.fori_loop(0, blocks, finish_step, 0, unroll=2)


def scratch(blocks, cells, near, list_width, near_width):
    return [
        pltpu.SMEM((blocks, list_width + 4), jnp.int32),
        pltpu.SMEM((blocks,), jnp.int32),
        pltpu.SMEM((blocks, near_width + 4), jnp.int32),
        pltpu.SMEM((blocks,), jnp.int32),
        pltpu.VMEM((cells + 1, 8, BLK), F32),
        pltpu.VMEM((cells + 1, 3 * ROWS, BLK), B16),
        pltpu.VMEM((near + 1, 8, BLK), F32),
        pltpu.VMEM((10 * cells, BLK), F32),
        pltpu.VMEM((ROWS * cells, BLK), F32),
    ]


def body(particles, tree_cells, let_list, let_count, part_list, cell_lists, near_lists):
    peers = lax.axis_size(("gx", "gy"))
    slots = let_list.shape[2]
    near_slots = part_list.shape[2]
    blocks, list_width = cell_lists.shape
    near_width = near_lists.shape[1]
    own_cells = tree_cells.shape[1] // BLK
    smem = pl.BlockSpec(memory_space=pltpu.SMEM)
    vmem = pl.BlockSpec(memory_space=pltpu.VMEM)
    params = pltpu.CompilerParams(vmem_limit_bytes=48 * 2**20)
    near_lists = jnp.transpose(near_lists)

    chosen = pl.pallas_call(
        pick_kernel,
        out_shape=jax.ShapeDtypeStruct((peers, 2 * slots + 1 + near_slots, 4, BLK), F32),
        in_specs=[smem, smem, smem, vmem, vmem],
        out_specs=vmem,
        compiler_params=params,
    )(jnp.transpose(let_list[0]), let_count, part_list[0], tree_cells, particles)
    moved = lax.all_to_all(chosen, ("gx", "gy"), split_axis=0, concat_axis=0, tiled=True)

    state = [
        jax.ShapeDtypeStruct((blocks, BLK, 6 * ROWS), B16),
        jax.ShapeDtypeStruct((blocks, 3, BLK, BLK), F32),
        jax.ShapeDtypeStruct((blocks, SUMS, BLK, BLK), F32),
        jax.ShapeDtypeStruct((blocks, BLK, BLK), F32),
    ]
    own = pl.pallas_call(
        own_kernel,
        out_shape=state,
        in_specs=[smem, smem, vmem, vmem],
        out_specs=[vmem] * len(state),
        scratch_shapes=scratch(blocks, own_cells, blocks, list_width, near_width),
        compiler_params=params,
        cost_estimate=pl.CostEstimate(flops=10**9, bytes_accessed=10**6, transcendentals=10**6),
    )(cell_lists, near_lists, particles, tree_cells)

    return pl.pallas_call(
        functools.partial(moved_kernel, own_cells, near_slots),
        out_shape=jax.ShapeDtypeStruct(particles.shape, F32),
        in_specs=[smem, smem] + [vmem] * (2 + len(state)),
        out_specs=vmem,
        scratch_shapes=scratch(
            blocks, peers * slots, len(near_offsets) * near_slots, list_width, near_width
        )
        + [pltpu.VMEM(leaf.shape, leaf.dtype) for leaf in state[2:]]
        + [pltpu.SMEM((own_cells + peers * slots,), jnp.int32)],
        compiler_params=params,
    )(cell_lists, near_lists, particles, *own, moved)


def solution(mesh):
    return jax.shard_map(
        body,
        mesh=mesh,
        in_specs=(
            P(None, ("gx", "gy")),
            P(None, ("gx", "gy")),
            P(("gx", "gy"), None, None),
            P(("gx", "gy"), None),
            P(("gx", "gy"), None, None),
            P(("gx", "gy"), None),
            P(("gx", "gy"), None),
        ),
        out_specs=P(None, ("gx", "gy")),
        check_vma=False,
    )
```

```python
import functools

import jax
import jax.numpy as jnp
from jax import lax
from jax.experimental import pallas as pl
from jax.experimental.pallas import tpu as pltpu
from jax.sharding import PartitionSpec as P

BLK = 128
ROWS = 16
SUMS = 4
SOFTENING = 0.0025
near_offsets = (1, -1, 2, -2)
F32 = jnp.float32
B16 = jnp.bfloat16


def at_block(index):
    return pl.ds(pl.multiple_of(index * BLK, BLK), BLK)


def split3(value):
    high = value.astype(B16)
    rest = value - high.astype(F32)
    middle = rest.astype(B16)
    low = (rest - middle.astype(F32)).astype(B16)
    return high, middle, low


def split2(value):
    high = value.astype(B16)
    return high, (value - high.astype(F32)).astype(B16)


def stack_rows(rows):
    sub = lax.broadcasted_iota(jnp.int32, (8, BLK), 0)
    out = rows[0]
    for i in range(1, len(rows)):
        out = jnp.where(sub == i, rows[i], out)
    return out


def wide(row):
    return jnp.broadcast_to(row, (8, BLK))


def quadrupole_rows(x, y, z, xx, yy, xy, xz, yz):
    xx, yy, xy, xz, yz = (2.5 * v for v in (xx, yy, xy, xz, yz))
    zz = -(xx + yy)
    qx = xx * x + xy * y + xz * z
    qy = xy * x + yy * y + yz * z
    qz = xz * x + yz * y + zz * z
    inner = qx * x + qy * y + qz * z
    return [qx, qy, qz, inner, xx, yy, zz, xy, yz, xz]


def target_rows(x, y, z):
    one = jnp.ones((8, BLK), F32)
    first = stack_rows([-2 * x, -2 * y, -2 * z, one, x * x, y * y, z * z, 2 * x * y])
    second = stack_rows([2 * y * z, 2 * x * z] + [jnp.zeros((8, BLK), F32)] * 6)
    return jnp.concatenate([first, second], axis=0)


def six(weights):
    high, middle, low = weights[0:ROWS], weights[ROWS : 2 * ROWS], weights[2 * ROWS :]
    return jnp.concatenate([high, high, high, middle, middle, low], axis=0)


def contract(left, right):
    return lax.dot_general(left, right, (((1,), (1,)), ((), ())), preferred_element_type=F32)


def fetch(sources, targets, arrived):
    copies = [
        pltpu.make_async_copy(source, target, arrived.at[i])
        for i, (source, target) in enumerate(zip(sources, targets))
    ]
    for copy in copies:
        copy.start()
    for copy in copies:
        copy.wait()


def pick_kernel(*refs):
    chosen = refs[5]
    let_list, let_count, part_list, cells, particles, arrived = refs[6:]
    fetch(refs[:5], refs[6:11], arrived)
    slots, peers = let_list.shape
    sub = lax.broadcasted_iota(jnp.int32, (4, BLK), 0)

    def peer_step(d, unused):
        count = let_count[0, d]
        for k in range(slots):
            columns = at_block(let_list[k, d])
            live = k < count
            chosen[d, k] = jnp.where(live, cells[0:4, columns], 0.0)
            quad = jnp.where(sub == 2, cells[8:9, columns], cells[4:8, columns])
            chosen[d, slots + k] = jnp.where(live, quad, 0.0)
            chosen[d, 2 * slots, k : k + 1, :] = jnp.where(live, cells[9:10, columns], 0.0)
        return unused

    lax.fori_loop(0, peers, peer_step, 0, unroll=4)
    for position, offset in enumerate(near_offsets):
        d = lax.axis_index(("gx", "gy")) + offset

        @pl.when((d >= 0) & (d < peers))
        def _():
            for k in range(part_list.shape[1]):
                chosen[d, 2 * slots + 1 + k] = particles[:, at_block(part_list[position, k])]


def put_eight(first, fields, rows):
    for i, value in enumerate(fields):
        rows[pl.ds(first * ROWS + i, 8, stride=ROWS), :] = value
    for i in range(len(fields), ROWS):
        rows[pl.ds(first * ROWS + i, 8, stride=ROWS), :] = jnp.zeros((8, BLK), F32)


def put_weights(count, rows, weights):
    def step(b, unused):
        high, middle, low = split3(rows[pl.ds(pl.multiple_of(b * ROWS, ROWS), ROWS), :])
        weights[b, 0:ROWS] = high
        weights[b, ROWS : 2 * ROWS] = middle
        weights[b, 2 * ROWS :] = low
        return unused

    lax.fori_loop(0, count, step, 0, unroll=8)


def cell_group(size, j, first, lists, targets, spread, places, weights, sums, quads):
    blocks = [lists[j, first + i] for i in range(size)]
    coefficients = jnp.concatenate([six(weights[b]) for b in blocks], axis=1)
    bent = jnp.dot(targets[j], coefficients, preferred_element_type=F32)
    left = []
    for low in range(0, BLK, 16):
        rows = slice(low, low + 16)
        x, y, z = (spread[j, f, rows] for f in range(3))
        ax, ay, az, potential = (sums[j, f, rows] for f in range(SUMS))
        parts = []
        for i, b in enumerate(blocks):
            rx, ry, rz = x - places[b, 0:1, :], y - places[b, 1:2, :], z - places[b, 2:3, :]
            inverse = lax.rsqrt(rx * rx + ry * ry + (rz * rz + SOFTENING))
            square = inverse * inverse
            fifth = square * square * inverse
            pulled = inverse * places[b, 3:4, :]
            radial = square * (pulled + bent[rows, i * BLK : (i + 1) * BLK] * fifth)
            ax += radial * rx
            ay += radial * ry
            az += radial * rz
            potential += pulled
            parts += split2(fifth)
        for f, value in enumerate((ax, ay, az, potential)):
            sums[j, f, rows] = value
        left.append(jnp.concatenate(parts, axis=1))
    right = jnp.concatenate([weights[b] for b in blocks for _ in range(2)], axis=1)
    quads[j, :, : 3 * ROWS] += contract(jnp.concatenate(left, axis=0), right)


def near_group(size, j, first, lists, spread, places, sums):
    blocks = [lists[j, first + i] for i in range(size)]
    for low in range(0, BLK, 16):
        rows = slice(low, low + 16)
        x, y, z = (spread[j, f, rows] for f in range(3))
        ax, ay, az, potential = (sums[j, f, rows] for f in range(SUMS))
        for b in blocks:
            rx, ry, rz = x - places[b, 0:1, :], y - places[b, 1:2, :], z - places[b, 2:3, :]
            inverse = lax.rsqrt(rx * rx + ry * ry + (rz * rz + SOFTENING))
            pulled = inverse * places[b, 3:4, :]
            radial = pulled * (inverse * inverse)
            ax += radial * rx
            ay += radial * ry
            az += radial * rz
            potential += pulled
        for f, value in enumerate((ax, ay, az, potential)):
            sums[j, f, rows] = value


def in_groups(count, group):
    fours = (count + 1) // 4

    def four(i, unused):
        group(4, 4 * i)
        return unused

    lax.fori_loop(0, fours, four, 0)

    @pl.when(4 * fours < count)
    def _():
        group(2, 4 * fours)


def keep_some(j, source, width, base, target, counts, live, nothing):
    count = jnp.int32(0)
    for l in range(width):
        index = source(j, l)
        target[j, count] = index - base
        count = count + live(index)
    for extra in range(3):
        target[j, count + extra] = nothing
    counts[j] = count


def selectors():
    shape = (ROWS, (3 + 2 * SUMS) * BLK)
    row = lax.broadcasted_iota(jnp.int32, shape, 0)
    lane = lax.broadcasted_iota(jnp.int32, shape, 1)
    inside = lane % BLK
    quad = (lane < 3 * BLK) & (inside < 3 * ROWS) & (inside % ROWS == row) & (row < 10)
    total = (lane >= 3 * BLK) & ((lane - 3 * BLK) // (2 * BLK) == row - (ROWS - SUMS))
    return jnp.where(quad | total, 1.0, 0.0).astype(B16)


def forces_of(j, chooser, particles, sums, quads):
    parts = list(split3(quads[j]))
    for f in range(SUMS):
        parts += split2(sums[j, f])
    mixed = contract(chooser, jnp.concatenate(parts, axis=1))
    qx, qy, qz, inner, xx, yy, zz, xy, yz, xz = (mixed[i : i + 1] for i in range(10))
    sx, sy, sz, pulls = (mixed[ROWS - SUMS + f : ROWS - SUMS + f + 1] for f in range(SUMS))
    x, y, z = (particles[f : f + 1, at_block(j)] for f in range(3))
    ax = xx * x + xy * y + xz * z
    ay = xy * x + yy * y + yz * z
    az = xz * x + yz * y + zz * z
    bent = ax * x + ay * y + az * z - 2 * (qx * x + qy * y + qz * z) + inner
    return (
        0.4 * (ax - qx) - sx,
        0.4 * (ay - qy) - sy,
        0.4 * (az - qz) - sz,
        -pulls - 0.2 * bent,
    )


def own_kernel(*refs):
    out, targets_out = refs[4:6]
    (lists, list_counts, near_kept, near_counts, places, weights, near_places, fields, rows) = refs[6:15]
    targets, spread, sums, quads, sent, cell_lists, near_lists, particles, cells, arrived = refs[15:]
    fetch(refs[:4], refs[20:24], arrived)
    blocks = cell_lists.shape[0]
    own_cells = cells.shape[1] // BLK

    def by_field(b, unused):
        fields[pl.ds(b, 8, stride=own_cells), :] = cells[0:8, at_block(b)]
        fields[pl.ds(8 * own_cells + b, 2, stride=own_cells), :] = cells[8:10, at_block(b)]
        places[b] = cells[0:8, at_block(b)]
        return unused

    lax.fori_loop(0, own_cells, by_field, 0, unroll=8)

    def eight(g, unused):
        first = pl.multiple_of(8 * g, 8)
        x, y, z, _, xx, yy, _, xy, xz, yz = (
            fields[pl.ds(f * own_cells + first, 8), :] for f in range(10)
        )
        put_eight(first, quadrupole_rows(x, y, z, xx, yy, xy, xz, yz), rows)
        return unused

    lax.fori_loop(0, own_cells // 8, eight, 0, unroll=2)
    put_weights(own_cells, rows, weights)
    weights[own_cells] = jnp.zeros((3 * ROWS, BLK), B16)
    places[own_cells] = jnp.zeros((8, BLK), F32)
    near_places[blocks] = jnp.zeros((8, BLK), F32)

    lane = lax.broadcasted_iota(jnp.int32, (BLK, BLK), 1)
    unit = jnp.where(lax.broadcasted_iota(jnp.int32, (BLK, BLK), 0) == lane, 1.0, 0.0).astype(B16)
    pick = coordinates()

    def prepare_target(j, unused):
        near_places[j, 0:4, :] = particles[:, at_block(j)]
        x, y, z = (wide(particles[f : f + 1, at_block(j)]) for f in range(3))
        high, middle, low = split3(target_rows(x, y, z))
        turned = contract(unit, jnp.concatenate([high, middle, low, high, middle, high], axis=0))
        turned = turned.astype(B16)
        targets[j] = turned
        begin_block(j, turned, pick, spread, sums, quads)
        keep_some(
            j, lambda j, l: cell_lists[j, l], cell_lists.shape[1], 0, lists, list_counts,
            lambda b: (b < own_cells).astype(jnp.int32), own_cells,
        )
        keep_some(
            j, lambda j, l: near_lists[l, j], near_lists.shape[0], 0, near_kept, near_counts,
            lambda b: (b < blocks).astype(jnp.int32), blocks,
        )
        return unused

    lax.fori_loop(0, blocks, prepare_target, 0, unroll=4)
    hand_on = pltpu.make_async_copy(targets, targets_out, sent.at[0])
    hand_on.start()
    add_all(
        blocks, lists, list_counts, near_kept, near_counts, targets, spread, places, weights,
        near_places, sums, quads,
    )
    chooser = selectors()

    def finish_step(j, unused):
        for f, row in enumerate(forces_of(j, chooser, particles, sums, quads)):
            out[f : f + 1, at_block(j)] = row
        return unused

    lax.fori_loop(0, blocks, finish_step, 0, unroll=4)
    hand_on.wait()


def coordinates():
    shape = (6 * ROWS, 3 * BLK)
    row = lax.broadcasted_iota(jnp.int32, shape, 0)
    axis = lax.broadcasted_iota(jnp.int32, shape, 1) // BLK
    return jnp.where((row % ROWS == axis) & (row < 3 * ROWS), -0.5, 0.0).astype(B16)


def begin_block(j, turned, pick, spread, sums, quads):
    wider = jnp.dot(turned, pick, preferred_element_type=F32)
    for f in range(3):
        spread[j, f] = wider[:, f * BLK : (f + 1) * BLK]
    for f in range(SUMS):
        sums[j, f] = jnp.zeros((BLK, BLK), F32)
    quads[j] = jnp.zeros((BLK, BLK), F32)


def add_all(
    blocks, lists, list_counts, near_kept, near_counts, targets, spread, places, weights,
    near_places, sums, quads,
):
    def block_step(j, unused):
        in_groups(
            list_counts[j],
            lambda size, first: cell_group(
                size, j, first, lists, targets, spread, places, weights, sums, quads
            ),
        )
        in_groups(
            near_counts[j],
            lambda size, first: near_group(size, j, first, near_kept, spread, near_places, sums),
        )
        return unused

    lax.fori_loop(0, blocks, block_step, 0)


def moved_kernel(own_cells, near_slots, *refs):
    out = refs[6]
    (lists, list_counts, near_kept, near_counts, places, weights, near_places, fields, rows) = refs[7:16]
    spread, sums, quads, live = refs[16:20]
    cell_lists, near_lists, particles, targets, partial, moved, arrived = refs[20:]
    fetch(refs[:6], refs[20:26], arrived)
    blocks = cell_lists.shape[0]
    peers, slots = moved.shape[0], moved.shape[2]
    count = peers * slots
    near_moved = len(near_offsets) * near_slots
    me = lax.axis_index(("gx", "gy"))

    def by_field(s, unused):
        for k in range(slots):
            b = s * slots + k
            fields[pl.ds(b, 4, stride=count), :] = moved[s, k]
            fields[pl.ds(4 * count + b, 4, stride=count), :] = moved[s, slots + k]
            places[b, 0:4, :] = moved[s, k]
        fields[pl.ds(8 * count + s * slots, slots), :] = moved[s, 2 * slots]
        return unused

    lax.fori_loop(0, peers, by_field, 0, unroll=2)

    def none_live(b, unused):
        live[b] = 0
        return unused

    lax.fori_loop(0, own_cells, none_live, 0, unroll=8)
    bit = lax.broadcasted_iota(jnp.int32, (8, BLK), 0)

    def eight(g, unused):
        first = pl.multiple_of(8 * g, 8)
        x, y, z, mass, xx, yy, xz, xy, yz = (
            fields[pl.ds(f * count + first, 8), :] for f in range(9)
        )
        put_eight(first, quadrupole_rows(x, y, z, xx, yy, xy, xz, yz), rows)
        some = (mass != 0) | (xx != 0) | (yy != 0) | (xy != 0) | (xz != 0) | (yz != 0)
        some = jnp.max(jnp.where(some, 1.0, 0.0), axis=1, keepdims=True)
        code = jnp.sum(some * jnp.left_shift(1, bit[:, 0:1]).astype(F32)).astype(jnp.int32)
        for i in range(8):
            live[own_cells + first + i] = jnp.right_shift(code, i) & 1
        return unused

    lax.fori_loop(0, count // 8, eight, 0, unroll=4)
    put_weights(count, rows, weights)
    weights[count] = jnp.zeros((3 * ROWS, BLK), B16)
    places[count] = jnp.zeros((8, BLK), F32)
    for position, offset in enumerate(near_offsets):
        source = me - offset
        there = (source >= 0) & (source < peers)
        safe = jnp.clip(source, 0, peers - 1)
        for k in range(near_slots):
            block = moved[safe, 2 * slots + 1 + k]
            near_places[position * near_slots + k, 0:4, :] = jnp.where(there, block, 0.0)
    near_places[near_moved] = jnp.zeros((8, BLK), F32)

    pick = coordinates()

    def prepare_target(j, unused):
        begin_block(j, targets[j], pick, spread, sums, quads)
        keep_some(
            j, lambda j, l: cell_lists[j, l], cell_lists.shape[1], own_cells, lists, list_counts,
            lambda b: live[b], count,
        )
        keep_some(
            j, lambda j, l: near_lists[l, j], near_lists.shape[0], blocks, near_kept, near_counts,
            lambda b: (b >= blocks).astype(jnp.int32), near_moved,
        )
        return unused

    lax.fori_loop(0, blocks, prepare_target, 0, unroll=4)
    add_all(
        blocks, lists, list_counts, near_kept, near_counts, targets, spread, places, weights,
        near_places, sums, quads,
    )

    chooser = selectors()

    def finish_step(j, unused):
        for f, row in enumerate(forces_of(j, chooser, particles, sums, quads)):
            out[f : f + 1, at_block(j)] = row + partial[f : f + 1, at_block(j)]
        return unused

    lax.fori_loop(0, blocks, finish_step, 0, unroll=4)


def scratch(blocks, cells, near, list_width, near_width):
    return [
        pltpu.SMEM((blocks, list_width + 4), jnp.int32),
        pltpu.SMEM((blocks,), jnp.int32),
        pltpu.SMEM((blocks, near_width + 4), jnp.int32),
        pltpu.SMEM((blocks,), jnp.int32),
        pltpu.VMEM((cells + 1, 8, BLK), F32),
        pltpu.VMEM((cells + 1, 3 * ROWS, BLK), B16),
        pltpu.VMEM((near + 1, 8, BLK), F32),
        pltpu.VMEM((10 * cells, BLK), F32),
        pltpu.VMEM((ROWS * cells, BLK), F32),
    ]


def body(particles, tree_cells, let_list, let_count, part_list, cell_lists, near_lists):
    peers = lax.axis_size(("gx", "gy"))
    slots = let_list.shape[2]
    near_slots = part_list.shape[2]
    blocks, list_width = cell_lists.shape
    near_width = near_lists.shape[1]
    own_cells = tree_cells.shape[1] // BLK
    far = pl.BlockSpec(memory_space=pltpu.HBM)
    vmem = pl.BlockSpec(memory_space=pltpu.VMEM)
    params = pltpu.CompilerParams(vmem_limit_bytes=60 * 2**20)

    def landing(numbers, arrays):
        spaces = [pltpu.SMEM(a.shape, a.dtype) for a in numbers]
        spaces += [pltpu.VMEM(a.shape, a.dtype) for a in arrays]
        return spaces + [pltpu.SemaphoreType.DMA((len(spaces),))]

    choice = [jnp.transpose(let_list[0]), let_count, part_list[0]]
    chosen = pl.pallas_call(
        pick_kernel,
        out_shape=jax.ShapeDtypeStruct((peers, 2 * slots + 1 + near_slots, 4, BLK), F32),
        in_specs=[far] * 5,
        out_specs=vmem,
        scratch_shapes=landing(choice, [tree_cells, particles]),
        compiler_params=params,
    )(*choice, tree_cells, particles)
    moved = lax.all_to_all(chosen, ("gx", "gy"), split_axis=0, concat_axis=0, tiled=True)

    numbers = [cell_lists, jnp.transpose(near_lists)]
    targets = jax.ShapeDtypeStruct((blocks, BLK, 6 * ROWS), B16)
    sums = [
        pltpu.VMEM((blocks, 3, BLK, BLK), F32),
        pltpu.VMEM((blocks, SUMS, BLK, BLK), F32),
        pltpu.VMEM((blocks, BLK, BLK), F32),
    ]
    partial, turned = pl.pallas_call(
        own_kernel,
        out_shape=[jax.ShapeDtypeStruct(particles.shape, F32), targets],
        in_specs=[far] * 4,
        out_specs=[vmem, far],
        scratch_shapes=scratch(blocks, own_cells, blocks, list_width, near_width)
        + [pltpu.VMEM(targets.shape, targets.dtype)]
        + sums
        + [pltpu.SemaphoreType.DMA((1,))]
        + landing(numbers, [particles, tree_cells]),
        compiler_params=params,
        cost_estimate=pl.CostEstimate(flops=10**9, bytes_accessed=10**6, transcendentals=10**6),
    )(*numbers, particles, tree_cells)

    return pl.pallas_call(
        functools.partial(moved_kernel, own_cells, near_slots),
        out_shape=jax.ShapeDtypeStruct(particles.shape, F32),
        in_specs=[far] * 6,
        out_specs=vmem,
        scratch_shapes=scratch(
            blocks, peers * slots, len(near_offsets) * near_slots, list_width, near_width
        )
        + sums
        + [pltpu.SMEM((own_cells + peers * slots,), jnp.int32)]
        + landing(numbers, [particles, turned, partial, moved]),
        compiler_params=params,
    )(*numbers, particles, turned, partial, moved)


def solution(mesh):
    return jax.shard_map(
        body,
        mesh=mesh,
        in_specs=(
            P(None, ("gx", "gy")),
            P(None, ("gx", "gy")),
            P(("gx", "gy"), None, None),
            P(("gx", "gy"), None),
            P(("gx", "gy"), None, None),
            P(("gx", "gy"), None),
            P(("gx", "gy"), None),
        ),
        out_specs=P(None, ("gx", "gy")),
        check_vma=False,
    )
```

```python
import functools

import jax
import jax.numpy as jnp
from jax import lax
from jax.experimental import pallas as pl
from jax.experimental.pallas import tpu as pltpu
from jax.sharding import PartitionSpec as P

BLK = 128
ROWS = 16
SUMS = 4
SOFTENING = 0.0025
near_offsets = (1, -1, 2, -2)
F32 = jnp.float32
B16 = jnp.bfloat16


def at_block(index):
    return pl.ds(pl.multiple_of(index * BLK, BLK), BLK)


def split3(value):
    high = value.astype(B16)
    rest = value - high.astype(F32)
    middle = rest.astype(B16)
    low = (rest - middle.astype(F32)).astype(B16)
    return high, middle, low


def split2(value):
    high = value.astype(B16)
    return high, (value - high.astype(F32)).astype(B16)


def stack_rows(rows):
    sub = lax.broadcasted_iota(jnp.int32, (8, BLK), 0)
    out = rows[0]
    for i in range(1, len(rows)):
        out = jnp.where(sub == i, rows[i], out)
    return out


def wide(row):
    return jnp.broadcast_to(row, (8, BLK))


def quadrupole_rows(x, y, z, xx, yy, xy, xz, yz):
    xx, yy, xy, xz, yz = (2.5 * v for v in (xx, yy, xy, xz, yz))
    zz = -(xx + yy)
    qx = xx * x + xy * y + xz * z
    qy = xy * x + yy * y + yz * z
    qz = xz * x + yz * y + zz * z
    inner = qx * x + qy * y + qz * z
    return [qx, qy, qz, inner, xx, yy, zz, xy, yz, xz]


def target_rows(x, y, z):
    one = jnp.ones((8, BLK), F32)
    first = stack_rows([-2 * x, -2 * y, -2 * z, one, x * x, y * y, z * z, 2 * x * y])
    second = stack_rows([2 * y * z, 2 * x * z] + [jnp.zeros((8, BLK), F32)] * 6)
    return jnp.concatenate([first, second], axis=0)


def six(weights):
    high, middle, low = weights[0:ROWS], weights[ROWS : 2 * ROWS], weights[2 * ROWS :]
    return jnp.concatenate([high, high, high, middle, middle, low], axis=0)


def contract(left, right):
    return lax.dot_general(left, right, (((1,), (1,)), ((), ())), preferred_element_type=F32)


def fetch(sources, targets, arrived):
    copies = [
        pltpu.make_async_copy(source, target, arrived.at[i])
        for i, (source, target) in enumerate(zip(sources, targets))
    ]
    for copy in copies:
        copy.start()
    return copies


def wait_for(copies):
    for copy in copies:
        copy.wait()


def pick_kernel(*refs):
    chosen = refs[5]
    let_list, let_count, part_list, cells, particles, arrived = refs[6:]
    wait_for(fetch(refs[:5], refs[6:11], arrived))
    slots, peers = let_list.shape
    sub = lax.broadcasted_iota(jnp.int32, (4, BLK), 0)

    def peer_step(d, unused):
        count = let_count[0, d]
        for k in range(slots):
            columns = at_block(let_list[k, d])
            live = k < count
            chosen[d, k] = jnp.where(live, cells[0:4, columns], 0.0)
            quad = jnp.where(sub == 2, cells[8:9, columns], cells[4:8, columns])
            chosen[d, slots + k] = jnp.where(live, quad, 0.0)
            chosen[d, 2 * slots, k : k + 1, :] = jnp.where(live, cells[9:10, columns], 0.0)
        return unused

    lax.fori_loop(0, peers, peer_step, 0, unroll=4)
    for position, offset in enumerate(near_offsets):
        d = lax.axis_index(("gx", "gy")) + offset

        @pl.when((d >= 0) & (d < peers))
        def _():
            for k in range(part_list.shape[1]):
                chosen[d, 2 * slots + 1 + k] = particles[:, at_block(part_list[position, k])]


def put_eight(first, fields, rows):
    for i, value in enumerate(fields):
        rows[pl.ds(first * ROWS + i, 8, stride=ROWS), :] = value
    for i in range(len(fields), ROWS):
        rows[pl.ds(first * ROWS + i, 8, stride=ROWS), :] = jnp.zeros((8, BLK), F32)


def put_weights(count, rows, weights):
    def step(b, unused):
        high, middle, low = split3(rows[pl.ds(pl.multiple_of(b * ROWS, ROWS), ROWS), :])
        weights[b, 0:ROWS] = high
        weights[b, ROWS : 2 * ROWS] = middle
        weights[b, 2 * ROWS :] = low
        return unused

    lax.fori_loop(0, count, step, 0, unroll=8)


def group(cells, near, j, first, near_first, lists, near_kept, targets, spread, places, weights,
          near_places, sums, quads):
    blocks = [lists[j, first + i] for i in range(cells)]
    near_blocks = [near_kept[j, near_first + i] for i in range(near)]
    if cells:
        coefficients = jnp.concatenate([six(weights[b]) for b in blocks], axis=1)
        bent = jnp.dot(targets[j], coefficients, preferred_element_type=F32)
    left = []
    for low in range(0, BLK, 16):
        rows = slice(low, low + 16)
        x, y, z = (spread[j, f, rows] for f in range(3))
        ax, ay, az, potential = (sums[j, f, rows] for f in range(SUMS))
        parts = []
        for i, (b, place) in enumerate(
            [(b, near_places) for b in near_blocks] + [(b, places) for b in blocks]
        ):
            rx, ry, rz = x - place[b, 0:1, :], y - place[b, 1:2, :], z - place[b, 2:3, :]
            inverse = lax.rsqrt(rx * rx + ry * ry + (rz * rz + SOFTENING))
            square = inverse * inverse
            pulled = inverse * place[b, 3:4, :]
            if i < near:
                radial = pulled * square
            else:
                fifth = square * square * inverse
                columns = slice((i - near) * BLK, (i - near + 1) * BLK)
                radial = square * (pulled + bent[rows, columns] * fifth)
                parts += split2(fifth)
            ax += radial * rx
            ay += radial * ry
            az += radial * rz
            potential += pulled
        for f, value in enumerate((ax, ay, az, potential)):
            sums[j, f, rows] = value
        if cells:
            left.append(jnp.concatenate(parts, axis=1))
    if cells:
        right = jnp.concatenate([weights[b] for b in blocks for _ in range(2)], axis=1)
        quads[j, :, : 3 * ROWS] += contract(jnp.concatenate(left, axis=0), right)


def add_block(j, count, near_count, *refs):
    fours = jnp.where(count >= 6, (count - 2) // 4, 0)
    fours = fours + (count - 4 * fours == 4).astype(jnp.int32)
    rest = count - 4 * fours

    def four(i, unused):
        group(4, 0, j, 4 * i, 0, *refs)
        return unused

    lax.fori_loop(0, fours, four, 0)
    for size, beside in ((1, 2), (2, 2), (3, 2), (5, 0)):

        @pl.when(rest == size)
        def _():
            group(size, beside, j, 4 * fours, 0, *refs)

    done = jnp.where((rest >= 1) & (rest <= 3), 2, 0)
    left = jnp.maximum(near_count - done, 0)
    near_fours = (left + 1) // 4

    def near_four(i, unused):
        group(0, 4, j, 0, done + 4 * i, *refs)
        return unused

    lax.fori_loop(0, near_fours, near_four, 0)

    @pl.when(4 * near_fours < left)
    def _():
        group(0, 2, j, 0, done + 4 * near_fours, *refs)


def keep_some(j, source, width, base, target, counts, live, nothing):
    count = jnp.int32(0)
    for l in range(width):
        index = source(j, l)
        target[j, count] = index - base
        count = count + live(index)
    for extra in range(3):
        target[j, count + extra] = nothing
    counts[j] = count


def selectors():
    shape = (ROWS, (3 + 2 * SUMS) * BLK)
    row = lax.broadcasted_iota(jnp.int32, shape, 0)
    lane = lax.broadcasted_iota(jnp.int32, shape, 1)
    inside = lane % BLK
    quad = (lane < 3 * BLK) & (inside < 3 * ROWS) & (inside % ROWS == row) & (row < 10)
    total = (lane >= 3 * BLK) & ((lane - 3 * BLK) // (2 * BLK) == row - (ROWS - SUMS))
    return jnp.where(quad | total, 1.0, 0.0).astype(B16)


def forces_of(j, chooser, particles, sums, quads):
    parts = list(split3(quads[j]))
    for f in range(SUMS):
        parts += split2(sums[j, f])
    mixed = contract(chooser, jnp.concatenate(parts, axis=1))
    qx, qy, qz, inner, xx, yy, zz, xy, yz, xz = (mixed[i : i + 1] for i in range(10))
    sx, sy, sz, pulls = (mixed[ROWS - SUMS + f : ROWS - SUMS + f + 1] for f in range(SUMS))
    x, y, z = (particles[f : f + 1, at_block(j)] for f in range(3))
    ax = xx * x + xy * y + xz * z
    ay = xy * x + yy * y + yz * z
    az = xz * x + yz * y + zz * z
    bent = ax * x + ay * y + az * z - 2 * (qx * x + qy * y + qz * z) + inner
    return (
        0.4 * (ax - qx) - sx,
        0.4 * (ay - qy) - sy,
        0.4 * (az - qz) - sz,
        -pulls - 0.2 * bent,
    )


def own_kernel(*refs):
    out, targets_out = refs[4:6]
    (lists, list_counts, near_kept, near_counts, places, weights, near_places, fields, rows) = refs[6:15]
    targets, spread, sums, quads, sent, cell_lists, near_lists, particles, cells, arrived = refs[15:]
    copies = fetch(refs[:4], refs[20:24], arrived)
    blocks = cell_lists.shape[0]
    own_cells = cells.shape[1] // BLK
    clear(sums, quads)
    wait_for(copies)

    def by_field(b, unused):
        fields[pl.ds(b, 8, stride=own_cells), :] = cells[0:8, at_block(b)]
        fields[pl.ds(8 * own_cells + b, 2, stride=own_cells), :] = cells[8:10, at_block(b)]
        places[b] = cells[0:8, at_block(b)]
        return unused

    lax.fori_loop(0, own_cells, by_field, 0, unroll=8)

    def eight(g, unused):
        first = pl.multiple_of(8 * g, 8)
        x, y, z, _, xx, yy, _, xy, xz, yz = (
            fields[pl.ds(f * own_cells + first, 8), :] for f in range(10)
        )
        put_eight(first, quadrupole_rows(x, y, z, xx, yy, xy, xz, yz), rows)
        return unused

    lax.fori_loop(0, own_cells // 8, eight, 0, unroll=2)
    put_weights(own_cells, rows, weights)
    weights[own_cells] = jnp.zeros((3 * ROWS, BLK), B16)
    places[own_cells] = jnp.zeros((8, BLK), F32)
    near_places[blocks] = jnp.zeros((8, BLK), F32)

    lane = lax.broadcasted_iota(jnp.int32, (BLK, BLK), 1)
    unit = jnp.where(lax.broadcasted_iota(jnp.int32, (BLK, BLK), 0) == lane, 1.0, 0.0).astype(B16)
    pick = coordinates()

    def prepare_target(j, unused):
        near_places[j, 0:4, :] = particles[:, at_block(j)]
        x, y, z = (wide(particles[f : f + 1, at_block(j)]) for f in range(3))
        high, middle, low = split3(target_rows(x, y, z))
        turned = contract(unit, jnp.concatenate([high, middle, low, high, middle, high], axis=0))
        turned = turned.astype(B16)
        targets[j] = turned
        begin_block(j, turned, pick, spread)
        keep_some(
            j, lambda j, l: cell_lists[j, l], cell_lists.shape[1], 0, lists, list_counts,
            lambda b: (b < own_cells).astype(jnp.int32), own_cells,
        )
        keep_some(
            j, lambda j, l: near_lists[l, j], near_lists.shape[0], 0, near_kept, near_counts,
            lambda b: (b < blocks).astype(jnp.int32), blocks,
        )
        return unused

    lax.fori_loop(0, blocks, prepare_target, 0, unroll=4)
    hand_on = pltpu.make_async_copy(targets, targets_out, sent.at[0])
    hand_on.start()
    add_all(
        blocks, lists, list_counts, near_kept, near_counts, targets, spread, places, weights,
        near_places, sums, quads,
    )
    chooser = selectors()

    def finish_step(j, unused):
        for f, row in enumerate(forces_of(j, chooser, particles, sums, quads)):
            out[f : f + 1, at_block(j)] = row
        return unused

    lax.fori_loop(0, blocks, finish_step, 0, unroll=4)
    hand_on.wait()


def coordinates():
    shape = (6 * ROWS, 3 * BLK)
    row = lax.broadcasted_iota(jnp.int32, shape, 0)
    axis = lax.broadcasted_iota(jnp.int32, shape, 1) // BLK
    return jnp.where((row % ROWS == axis) & (row < 3 * ROWS), -0.5, 0.0).astype(B16)


def begin_block(j, turned, pick, spread):
    wider = jnp.dot(turned, pick, preferred_element_type=F32)
    for f in range(3):
        spread[j, f] = wider[:, f * BLK : (f + 1) * BLK]


def clear(sums, quads):
    def step(j, unused):
        for f in range(SUMS):
            sums[j, f] = jnp.zeros((BLK, BLK), F32)
        quads[j] = jnp.zeros((BLK, BLK), F32)
        return unused

    lax.fori_loop(0, quads.shape[0], step, 0)


def add_all(
    blocks, lists, list_counts, near_kept, near_counts, targets, spread, places, weights,
    near_places, sums, quads,
):
    def block_step(j, unused):
        add_block(
            j, list_counts[j], near_counts[j], lists, near_kept, targets, spread, places, weights,
            near_places, sums, quads,
        )
        return unused

    lax.fori_loop(0, blocks, block_step, 0)


def moved_kernel(own_cells, near_slots, *refs):
    out = refs[6]
    (lists, list_counts, near_kept, near_counts, places, weights, near_places, fields, rows) = refs[7:16]
    spread, sums, quads, live = refs[16:20]
    cell_lists, near_lists, particles, targets, partial, moved, arrived = refs[20:]
    copies = fetch(refs[:6], refs[20:26], arrived)
    blocks = cell_lists.shape[0]
    peers, slots = moved.shape[0], moved.shape[2]
    count = peers * slots
    near_moved = len(near_offsets) * near_slots
    me = lax.axis_index(("gx", "gy"))
    clear(sums, quads)

    def none_live(b, unused):
        live[b] = 0
        return unused

    lax.fori_loop(0, own_cells, none_live, 0, unroll=8)
    wait_for(copies)

    def by_field(s, unused):
        for k in range(slots):
            b = s * slots + k
            fields[pl.ds(b, 4, stride=count), :] = moved[s, k]
            fields[pl.ds(4 * count + b, 4, stride=count), :] = moved[s, slots + k]
            places[b, 0:4, :] = moved[s, k]
        fields[pl.ds(8 * count + s * slots, slots), :] = moved[s, 2 * slots]
        return unused

    lax.fori_loop(0, peers, by_field, 0, unroll=4)

    bit = lax.broadcasted_iota(jnp.int32, (8, BLK), 0)

    def eight(g, unused):
        first = pl.multiple_of(8 * g, 8)
        x, y, z, mass, xx, yy, xz, xy, yz = (
            fields[pl.ds(f * count + first, 8), :] for f in range(9)
        )
        put_eight(first, quadrupole_rows(x, y, z, xx, yy, xy, xz, yz), rows)
        some = (mass != 0) | (xx != 0) | (yy != 0) | (xy != 0) | (xz != 0) | (yz != 0)
        some = jnp.max(jnp.where(some, 1.0, 0.0), axis=1, keepdims=True)
        code = jnp.sum(some * jnp.left_shift(1, bit[:, 0:1]).astype(F32)).astype(jnp.int32)
        for i in range(8):
            live[own_cells + first + i] = jnp.right_shift(code, i) & 1
        return unused

    lax.fori_loop(0, count // 8, eight, 0, unroll=8)
    put_weights(count, rows, weights)
    weights[count] = jnp.zeros((3 * ROWS, BLK), B16)
    places[count] = jnp.zeros((8, BLK), F32)
    for position, offset in enumerate(near_offsets):
        source = me - offset
        there = (source >= 0) & (source < peers)
        safe = jnp.clip(source, 0, peers - 1)
        for k in range(near_slots):
            block = moved[safe, 2 * slots + 1 + k]
            near_places[position * near_slots + k, 0:4, :] = jnp.where(there, block, 0.0)
    near_places[near_moved] = jnp.zeros((8, BLK), F32)

    pick = coordinates()

    def prepare_target(j, unused):
        begin_block(j, targets[j], pick, spread)
        keep_some(
            j, lambda j, l: cell_lists[j, l], cell_lists.shape[1], own_cells, lists, list_counts,
            lambda b: live[b], count,
        )
        keep_some(
            j, lambda j, l: near_lists[l, j], near_lists.shape[0], blocks, near_kept, near_counts,
            lambda b: (b >= blocks).astype(jnp.int32), near_moved,
        )
        return unused

    lax.fori_loop(0, blocks, prepare_target, 0, unroll=4)
    add_all(
        blocks, lists, list_counts, near_kept, near_counts, targets, spread, places, weights,
        near_places, sums, quads,
    )

    chooser = selectors()

    def finish_step(j, unused):
        for f, row in enumerate(forces_of(j, chooser, particles, sums, quads)):
            out[f : f + 1, at_block(j)] = row + partial[f : f + 1, at_block(j)]
        return unused

    lax.fori_loop(0, blocks, finish_step, 0, unroll=4)


def scratch(blocks, cells, near, list_width, near_width):
    return [
        pltpu.SMEM((blocks, list_width + 4), jnp.int32),
        pltpu.SMEM((blocks,), jnp.int32),
        pltpu.SMEM((blocks, near_width + 4), jnp.int32),
        pltpu.SMEM((blocks,), jnp.int32),
        pltpu.VMEM((cells + 1, 8, BLK), F32),
        pltpu.VMEM((cells + 1, 3 * ROWS, BLK), B16),
        pltpu.VMEM((near + 1, 8, BLK), F32),
        pltpu.VMEM((10 * cells, BLK), F32),
        pltpu.VMEM((ROWS * cells, BLK), F32),
    ]


def body(particles, tree_cells, let_list, let_count, part_list, cell_lists, near_lists):
    peers = lax.axis_size(("gx", "gy"))
    slots = let_list.shape[2]
    near_slots = part_list.shape[2]
    blocks, list_width = cell_lists.shape
    near_width = near_lists.shape[1]
    own_cells = tree_cells.shape[1] // BLK
    far = pl.BlockSpec(memory_space=pltpu.HBM)
    vmem = pl.BlockSpec(memory_space=pltpu.VMEM)
    params = pltpu.CompilerParams(vmem_limit_bytes=60 * 2**20)

    def landing(numbers, arrays):
        spaces = [pltpu.SMEM(a.shape, a.dtype) for a in numbers]
        spaces += [pltpu.VMEM(a.shape, a.dtype) for a in arrays]
        return spaces + [pltpu.SemaphoreType.DMA((len(spaces),))]

    choice = [jnp.transpose(let_list[0]), let_count, part_list[0]]
    chosen = pl.pallas_call(
        pick_kernel,
        out_shape=jax.ShapeDtypeStruct((peers, 2 * slots + 1 + near_slots, 4, BLK), F32),
        in_specs=[far] * 5,
        out_specs=vmem,
        scratch_shapes=landing(choice, [tree_cells, particles]),
        compiler_params=params,
    )(*choice, tree_cells, particles)
    moved = lax.all_to_all(chosen, ("gx", "gy"), split_axis=0, concat_axis=0, tiled=True)

    numbers = [cell_lists, jnp.transpose(near_lists)]
    targets = jax.ShapeDtypeStruct((blocks, BLK, 6 * ROWS), B16)
    sums = [
        pltpu.VMEM((blocks, 3, BLK, BLK), F32),
        pltpu.VMEM((blocks, SUMS, BLK, BLK), F32),
        pltpu.VMEM((blocks, BLK, BLK), F32),
    ]
    partial, turned = pl.pallas_call(
        own_kernel,
        out_shape=[jax.ShapeDtypeStruct(particles.shape, F32), targets],
        in_specs=[far] * 4,
        out_specs=[vmem, far],
        scratch_shapes=scratch(blocks, own_cells, blocks, list_width, near_width)
        + [pltpu.VMEM(targets.shape, targets.dtype)]
        + sums
        + [pltpu.SemaphoreType.DMA((1,))]
        + landing(numbers, [particles, tree_cells]),
        compiler_params=pltpu.CompilerParams(vmem_limit_bytes=127 * 2**19),
        cost_estimate=pl.CostEstimate(flops=10**9, bytes_accessed=10**6, transcendentals=10**6),
    )(*numbers, particles, tree_cells)

    return pl.pallas_call(
        functools.partial(moved_kernel, own_cells, near_slots),
        out_shape=jax.ShapeDtypeStruct(particles.shape, F32),
        in_specs=[far] * 6,
        out_specs=vmem,
        scratch_shapes=scratch(
            blocks, peers * slots, len(near_offsets) * near_slots, list_width, near_width
        )
        + sums
        + [pltpu.SMEM((own_cells + peers * slots,), jnp.int32)]
        + landing(numbers, [particles, turned, partial, moved]),
        compiler_params=params,
    )(*numbers, particles, turned, partial, moved)


def solution(mesh):
    return jax.shard_map(
        body,
        mesh=mesh,
        in_specs=(
            P(None, ("gx", "gy")),
            P(None, ("gx", "gy")),
            P(("gx", "gy"), None, None),
            P(("gx", "gy"), None),
            P(("gx", "gy"), None, None),
            P(("gx", "gy"), None),
            P(("gx", "gy"), None),
        ),
        out_specs=P(None, ("gx", "gy")),
        check_vma=False,
    )
```

```python
import functools

import jax
import jax.numpy as jnp
from jax import lax
from jax.experimental import pallas as pl
from jax.experimental.pallas import tpu as pltpu
from jax.sharding import PartitionSpec as P

BLK = 128
ROWS = 16
SUMS = 4
SOFTENING = 0.0025
near_offsets = (1, -1, 2, -2)
F32 = jnp.float32
B16 = jnp.bfloat16


def at_block(index):
    return pl.ds(pl.multiple_of(index * BLK, BLK), BLK)


def split3(value):
    high = value.astype(B16)
    rest = value - high.astype(F32)
    middle = rest.astype(B16)
    low = (rest - middle.astype(F32)).astype(B16)
    return high, middle, low


def split2(value):
    high = value.astype(B16)
    return high, (value - high.astype(F32)).astype(B16)


def stack_rows(rows):
    sub = lax.broadcasted_iota(jnp.int32, (8, BLK), 0)
    out = rows[0]
    for i in range(1, len(rows)):
        out = jnp.where(sub == i, rows[i], out)
    return out


def wide(row):
    return jnp.broadcast_to(row, (8, BLK))


def quadrupole_rows(x, y, z, xx, yy, xy, xz, yz):
    xx, yy, xy, xz, yz = (2.5 * v for v in (xx, yy, xy, xz, yz))
    zz = -(xx + yy)
    qx = xx * x + xy * y + xz * z
    qy = xy * x + yy * y + yz * z
    qz = xz * x + yz * y + zz * z
    inner = qx * x + qy * y + qz * z
    return [qx, qy, qz, inner, xx, yy, zz, xy, yz, xz]


def target_rows(x, y, z):
    one = jnp.ones((8, BLK), F32)
    first = stack_rows([-2 * x, -2 * y, -2 * z, one, x * x, y * y, z * z, 2 * x * y])
    second = stack_rows([2 * y * z, 2 * x * z] + [jnp.zeros((8, BLK), F32)] * 6)
    return jnp.concatenate([first, second], axis=0)


def six(weights):
    high, middle, low = weights[0:ROWS], weights[ROWS : 2 * ROWS], weights[2 * ROWS :]
    return jnp.concatenate([high, high, high, middle, middle, low], axis=0)


def contract(left, right):
    return lax.dot_general(left, right, (((1,), (1,)), ((), ())), preferred_element_type=F32)


def fetch(sources, targets, arrived):
    copies = [
        pltpu.make_async_copy(source, target, arrived.at[i])
        for i, (source, target) in enumerate(zip(sources, targets))
    ]
    for copy in copies:
        copy.start()
    return copies


def wait_for(copies):
    for copy in copies:
        copy.wait()


def pick_kernel(*refs):
    chosen_out = refs[5]
    chosen, sent, let_list, let_count, part_list, cells, particles, arrived = refs[6:]
    wait_for(fetch(refs[:5], refs[8:13], arrived))
    slots, peers = let_list.shape
    sub = lax.broadcasted_iota(jnp.int32, (4, BLK), 0)

    def peer_step(d, unused):
        count = let_count[0, d]
        for k in range(slots):
            columns = at_block(let_list[k, d])
            live = k < count
            chosen[d, k] = jnp.where(live, cells[0:4, columns], 0.0)
            quad = jnp.where(sub == 2, cells[8:9, columns], cells[4:8, columns])
            chosen[d, slots + k] = jnp.where(live, quad, 0.0)
            chosen[d, 2 * slots, k : k + 1, :] = jnp.where(live, cells[9:10, columns], 0.0)
        return unused

    for position, offset in enumerate(near_offsets):
        d = lax.axis_index(("gx", "gy")) + offset

        @pl.when((d >= 0) & (d < peers))
        def _():
            for k in range(part_list.shape[1]):
                chosen[d, 2 * slots + 1 + k] = particles[:, at_block(part_list[position, k])]

    chunks = sent.shape[0]
    copies = []
    for c in range(chunks):
        part = slice(c * peers // chunks, (c + 1) * peers // chunks)
        lax.fori_loop(part.start, part.stop, peer_step, 0, unroll=4)
        copies.append(pltpu.make_async_copy(chosen.at[part], chosen_out.at[part], sent.at[c]))
        copies[-1].start()
    wait_for(copies)


def put_eight(first, fields, rows):
    for i, value in enumerate(fields):
        rows[pl.ds(first * ROWS + i, 8, stride=ROWS), :] = value
    for i in range(len(fields), ROWS):
        rows[pl.ds(first * ROWS + i, 8, stride=ROWS), :] = jnp.zeros((8, BLK), F32)


def put_weights(b, rows, weights):
    high, middle, low = split3(rows[pl.ds(pl.multiple_of(b * ROWS, ROWS), ROWS), :])
    weights[b, 0:ROWS] = high
    weights[b, ROWS : 2 * ROWS] = middle
    weights[b, 2 * ROWS :] = low


def group(cells, near, j, first, near_first, lists, near_kept, targets, spread, places, weights,
          near_places, sums, quads):
    blocks = [lists[j, first + i] for i in range(cells)]
    near_blocks = [near_kept[j, near_first + i] for i in range(near)]
    if cells:
        coefficients = jnp.concatenate([six(weights[b]) for b in blocks], axis=1)
        bent = jnp.dot(targets[j], coefficients, preferred_element_type=F32)
    left = []
    for low in range(0, BLK, 16):
        rows = slice(low, low + 16)
        x, y, z = (spread[j, f, rows] for f in range(3))
        ax, ay, az, potential = (sums[j, f, rows] for f in range(SUMS))
        parts = []
        for i, (b, place) in enumerate(
            [(b, near_places) for b in near_blocks] + [(b, places) for b in blocks]
        ):
            rx, ry, rz = x - place[b, 0:1, :], y - place[b, 1:2, :], z - place[b, 2:3, :]
            inverse = lax.rsqrt(rx * rx + ry * ry + (rz * rz + SOFTENING))
            square = inverse * inverse
            pulled = inverse * place[b, 3:4, :]
            if i < near:
                radial = pulled * square
            else:
                fifth = square * square * inverse
                columns = slice((i - near) * BLK, (i - near + 1) * BLK)
                radial = square * (pulled + bent[rows, columns] * fifth)
                parts += split2(fifth)
            ax += radial * rx
            ay += radial * ry
            az += radial * rz
            potential += pulled
        for f, value in enumerate((ax, ay, az, potential)):
            sums[j, f, rows] = value
        if cells:
            left.append(jnp.concatenate(parts, axis=1))
    if cells:
        right = jnp.concatenate([weights[b] for b in blocks for _ in range(2)], axis=1)
        quads[j, :, : 3 * ROWS] += contract(jnp.concatenate(left, axis=0), right)


def add_block(j, count, near_count, list_next, *refs):
    fours = jnp.where(count >= 6, (count - 2) // 4, 0)
    fours = fours + (count - 4 * fours == 4).astype(jnp.int32)
    rest = count - 4 * fours

    def four(i, unused):
        group(4, 0, j, 4 * i, 0, *refs)
        return unused

    lax.fori_loop(0, fours, four, 0)
    for size, beside in ((1, 2), (2, 2), (3, 2), (5, 0)):

        @pl.when(rest == size)
        def _():
            group(size, beside, j, 4 * fours, 0, *refs)
            list_next()

    pl.when(rest == 0)(list_next)
    done = jnp.where((rest >= 1) & (rest <= 3), 2, 0)
    left = jnp.maximum(near_count - done, 0)
    near_fours = (left + 1) // 4

    def near_four(i, unused):
        group(0, 4, j, 0, done + 4 * i, *refs)
        return unused

    lax.fori_loop(0, near_fours, near_four, 0)

    @pl.when(4 * near_fours < left)
    def _():
        group(0, 2, j, 0, done + 4 * near_fours, *refs)


def keep_some(j, source, width, base, target, counts, live, nothing):
    count = jnp.int32(0)
    for l in range(width):
        index = source(j, l)
        target[j, count] = index - base
        count = count + live(index)
    for extra in range(3):
        target[j, count + extra] = nothing
    counts[j] = count


def selectors():
    shape = (ROWS, 7 * BLK)
    row = lax.broadcasted_iota(jnp.int32, shape, 0)
    lane = lax.broadcasted_iota(jnp.int32, shape, 1)
    inside = lane % BLK
    quad = (lane < 3 * BLK) & (inside < 3 * ROWS) & (inside % ROWS == row) & (row < 10)
    half = 2 * ((lane - 3 * BLK) // (2 * BLK)) + (inside >= BLK // 2).astype(jnp.int32)
    total = (lane >= 3 * BLK) & (half == row - (ROWS - SUMS))
    return jnp.where(quad | total, 1.0, 0.0).astype(B16)


def fold(first, second):
    low = lax.broadcasted_iota(jnp.int32, first.shape, 1) < BLK // 2
    return jnp.where(low, first, second) + pltpu.roll(jnp.where(low, second, first), BLK // 2, 1)


def forces_of(j, chooser, particles, sums, quads):
    parts = list(split3(quads[j]))
    for f in range(0, SUMS, 2):
        parts += split2(fold(sums[j, f], sums[j, f + 1]))
    mixed = contract(chooser, jnp.concatenate(parts, axis=1))
    qx, qy, qz, inner, xx, yy, zz, xy, yz, xz = (mixed[i : i + 1] for i in range(10))
    sx, sy, sz, pulls = (mixed[ROWS - SUMS + f : ROWS - SUMS + f + 1] for f in range(SUMS))
    x, y, z = (particles[f : f + 1, at_block(j)] for f in range(3))
    ax = xx * x + xy * y + xz * z
    ay = xy * x + yy * y + yz * z
    az = xz * x + yz * y + zz * z
    bent = ax * x + ay * y + az * z - 2 * (qx * x + qy * y + qz * z) + inner
    return (
        0.4 * (ax - qx) - sx,
        0.4 * (ay - qy) - sy,
        0.4 * (az - qz) - sz,
        -pulls - 0.2 * bent,
    )


def own_kernel(*refs):
    out, targets_out, spread_out = refs[4:7]
    (lists, list_counts, near_kept, near_counts, places, weights, near_places, fields, rows) = refs[7:16]
    targets, spread, sums, quads, sent, cell_lists, near_lists, particles, cells, arrived = refs[16:]
    copies = fetch(refs[:4], refs[21:25], arrived)
    blocks = cell_lists.shape[0]
    own_cells = cells.shape[1] // BLK
    clear(sums, quads)
    wait_for(copies)

    def by_field(b, unused):
        fields[pl.ds(b, 8, stride=own_cells), :] = cells[0:8, at_block(b)]
        fields[pl.ds(8 * own_cells + b, 2, stride=own_cells), :] = cells[8:10, at_block(b)]
        places[b] = cells[0:8, at_block(b)]
        return unused

    lax.fori_loop(0, own_cells, by_field, 0, unroll=8)

    def eight(g, unused):
        first = pl.multiple_of(8 * g, 8)
        x, y, z, _, xx, yy, _, xy, xz, yz = (
            fields[pl.ds(f * own_cells + first, 8), :] for f in range(10)
        )
        put_eight(first, quadrupole_rows(x, y, z, xx, yy, xy, xz, yz), rows)
        return unused

    lax.fori_loop(0, own_cells // 8, eight, 0, unroll=2)

    def step(b, unused):
        put_weights(b, rows, weights)
        return unused

    lax.fori_loop(0, own_cells, step, 0, unroll=8)
    weights[own_cells] = jnp.zeros((3 * ROWS, BLK), B16)
    places[own_cells] = jnp.zeros((8, BLK), F32)
    near_places[blocks] = jnp.zeros((8, BLK), F32)

    lane = lax.broadcasted_iota(jnp.int32, (BLK, BLK), 1)
    unit = jnp.where(lax.broadcasted_iota(jnp.int32, (BLK, BLK), 0) == lane, 1.0, 0.0).astype(B16)
    pick = coordinates()

    def prepare_target(j, unused):
        near_places[j, 0:4, :] = particles[:, at_block(j)]
        x, y, z = (wide(particles[f : f + 1, at_block(j)]) for f in range(3))
        high, middle, low = split3(target_rows(x, y, z))
        turned = contract(unit, jnp.concatenate([high, middle, low, high, middle, high], axis=0))
        turned = turned.astype(B16)
        targets[j] = turned
        begin_block(j, turned, pick, spread)
        return unused

    lax.fori_loop(0, blocks, prepare_target, 0, unroll=4)

    def make_lists(j):
        keep_some(
            j, lambda j, l: cell_lists[j, l], cell_lists.shape[1], 0, lists, list_counts,
            lambda b: (b < own_cells).astype(jnp.int32), own_cells,
        )
        keep_some(
            j, lambda j, l: near_lists[l, j], near_lists.shape[0], 0, near_kept, near_counts,
            lambda b: (b < blocks).astype(jnp.int32), blocks,
        )

    hand_on = fetch([targets, spread], [targets_out, spread_out], sent)
    add_all(
        blocks, make_lists, lists, list_counts, near_kept, near_counts, targets, spread, places, weights,
        near_places, sums, quads,
    )
    chooser = selectors()

    def finish_step(j, unused):
        for f, row in enumerate(forces_of(j, chooser, particles, sums, quads)):
            out[f : f + 1, at_block(j)] = row
        return unused

    lax.fori_loop(0, blocks, finish_step, 0, unroll=4)
    wait_for(hand_on)


def coordinates():
    shape = (6 * ROWS, 3 * BLK)
    row = lax.broadcasted_iota(jnp.int32, shape, 0)
    axis = lax.broadcasted_iota(jnp.int32, shape, 1) // BLK
    return jnp.where((row % ROWS == axis) & (row < 3 * ROWS), -0.5, 0.0).astype(B16)


def begin_block(j, turned, pick, spread):
    wider = jnp.dot(turned, pick, preferred_element_type=F32)
    for f in range(3):
        spread[j, f] = wider[:, f * BLK : (f + 1) * BLK]


def clear(sums, quads):
    def step(j, unused):
        for f in range(SUMS):
            sums[j, f] = jnp.zeros((BLK, BLK), F32)
        quads[j] = jnp.zeros((BLK, BLK), F32)
        return unused

    lax.fori_loop(0, quads.shape[0], step, 0)


def add_all(
    blocks, make_lists, lists, list_counts, near_kept, near_counts, targets, spread, places, weights,
    near_places, sums, quads,
):
    make_lists(0)

    def block_step(j, unused):
        add_block(
            j, list_counts[j], near_counts[j], lambda: make_lists(jnp.minimum(j + 1, blocks - 1)),
            lists, near_kept, targets, spread, places, weights, near_places, sums, quads,
        )
        return unused

    lax.fori_loop(0, blocks, block_step, 0)


def moved_kernel(own_cells, near_slots, *refs):
    out = refs[7]
    (lists, list_counts, near_kept, near_counts, places, weights, near_places, fields, rows) = refs[8:17]
    sums, quads, live = refs[17:20]
    cell_lists, near_lists, moved, particles, targets, spread, partial, arrived = refs[20:]
    copies = fetch(refs[:7], refs[20:27], arrived)
    blocks = cell_lists.shape[0]
    peers, slots = moved.shape[0], moved.shape[2]
    count = peers * slots
    near_moved = len(near_offsets) * near_slots
    me = lax.axis_index(("gx", "gy"))
    clear(sums, quads)

    def none_live(b, unused):
        live[b] = 0
        return unused

    lax.fori_loop(0, own_cells, none_live, 0, unroll=8)
    wait_for(copies[:3])

    def by_field(s, unused):
        for k in range(slots):
            b = s * slots + k
            fields[pl.ds(b, 4, stride=count), :] = moved[s, k]
            fields[pl.ds(4 * count + b, 4, stride=count), :] = moved[s, slots + k]
            places[b, 0:4, :] = moved[s, k]
        fields[pl.ds(8 * count + s * slots, slots), :] = moved[s, 2 * slots]
        return unused

    lax.fori_loop(0, peers, by_field, 0, unroll=4)

    bit = lax.broadcasted_iota(jnp.int32, (8, BLK), 0)

    def eight(g, unused):
        first = pl.multiple_of(8 * g, 8)
        x, y, z, mass, xx, yy, xz, xy, yz = (
            fields[pl.ds(f * count + first, 8), :] for f in range(9)
        )
        put_eight(first, quadrupole_rows(x, y, z, xx, yy, xy, xz, yz), rows)
        some = (mass != 0) | (xx != 0) | (yy != 0) | (xy != 0) | (xz != 0) | (yz != 0)
        some = jnp.max(jnp.where(some, 1.0, 0.0), axis=1, keepdims=True)
        code = jnp.sum(some * jnp.left_shift(1, bit[:, 0:1]).astype(F32)).astype(jnp.int32)
        for i in range(8):
            live[own_cells + first + i] = jnp.right_shift(code, i) & 1
        return unused

    lax.fori_loop(0, count // 8, eight, 0, unroll=8)
    weights[count] = jnp.zeros((3 * ROWS, BLK), B16)
    places[count] = jnp.zeros((8, BLK), F32)
    for position, offset in enumerate(near_offsets):
        source = me - offset
        there = (source >= 0) & (source < peers)
        safe = jnp.clip(source, 0, peers - 1)
        for k in range(near_slots):
            block = moved[safe, 2 * slots + 1 + k]
            near_places[position * near_slots + k, 0:4, :] = jnp.where(there, block, 0.0)
    near_places[near_moved] = jnp.zeros((8, BLK), F32)

    def step(b, unused):
        put_weights(b, rows, weights)
        return unused

    lax.fori_loop(0, count, step, 0, unroll=8)

    def make_lists(j):
        keep_some(
            j, lambda j, l: cell_lists[j, l], cell_lists.shape[1], own_cells, lists, list_counts,
            lambda b: live[b], count,
        )
        keep_some(
            j, lambda j, l: near_lists[l, j], near_lists.shape[0], blocks, near_kept, near_counts,
            lambda b: (b >= blocks).astype(jnp.int32), near_moved,
        )

    wait_for(copies[3:])
    add_all(
        blocks, make_lists, lists, list_counts, near_kept, near_counts, targets, spread, places, weights,
        near_places, sums, quads,
    )

    chooser = selectors()

    def finish_step(j, unused):
        for f, row in enumerate(forces_of(j, chooser, particles, sums, quads)):
            out[f : f + 1, at_block(j)] = row + partial[f : f + 1, at_block(j)]
        return unused

    lax.fori_loop(0, blocks, finish_step, 0, unroll=4)


def scratch(blocks, cells, near, list_width, near_width):
    return [
        pltpu.SMEM((blocks, list_width + 4), jnp.int32),
        pltpu.SMEM((blocks,), jnp.int32),
        pltpu.SMEM((blocks, near_width + 4), jnp.int32),
        pltpu.SMEM((blocks,), jnp.int32),
        pltpu.VMEM((cells + 1, 8, BLK), F32),
        pltpu.VMEM((cells + 1, 3 * ROWS, BLK), B16),
        pltpu.VMEM((near + 1, 8, BLK), F32),
        pltpu.VMEM((10 * cells, BLK), F32),
        pltpu.VMEM((ROWS * cells, BLK), F32),
    ]


def body(particles, tree_cells, let_list, let_count, part_list, cell_lists, near_lists):
    peers = lax.axis_size(("gx", "gy"))
    slots = let_list.shape[2]
    near_slots = part_list.shape[2]
    blocks, list_width = cell_lists.shape
    near_width = near_lists.shape[1]
    own_cells = tree_cells.shape[1] // BLK
    far = pl.BlockSpec(memory_space=pltpu.HBM)
    vmem = pl.BlockSpec(memory_space=pltpu.VMEM)
    params = pltpu.CompilerParams(vmem_limit_bytes=60 * 2**20)

    def landing(numbers, arrays):
        spaces = [pltpu.SMEM(a.shape, a.dtype) for a in numbers]
        spaces += [pltpu.VMEM(a.shape, a.dtype) for a in arrays]
        return spaces + [pltpu.SemaphoreType.DMA((len(spaces),))]

    choice = [jnp.transpose(let_list[0]), let_count, part_list[0]]
    chosen = pl.pallas_call(
        pick_kernel,
        out_shape=jax.ShapeDtypeStruct((peers, 2 * slots + 1 + near_slots, 4, BLK), F32),
        in_specs=[far] * 5,
        out_specs=far,
        scratch_shapes=[
            pltpu.VMEM((peers, 2 * slots + 1 + near_slots, 4, BLK), F32),
            pltpu.SemaphoreType.DMA((4,)),
        ]
        + landing(choice, [tree_cells, particles]),
        compiler_params=params,
    )(*choice, tree_cells, particles)
    moved = lax.all_to_all(chosen, ("gx", "gy"), split_axis=0, concat_axis=0, tiled=True)

    numbers = [cell_lists, jnp.transpose(near_lists)]
    turned = [
        jax.ShapeDtypeStruct((blocks, BLK, 6 * ROWS), B16),
        jax.ShapeDtypeStruct((blocks, 3, BLK, BLK), F32),
    ]
    sums = [pltpu.VMEM((blocks, SUMS, BLK, BLK), F32), pltpu.VMEM((blocks, BLK, BLK), F32)]
    partial, *turned = pl.pallas_call(
        own_kernel,
        out_shape=[jax.ShapeDtypeStruct(particles.shape, F32)] + turned,
        in_specs=[far] * 4,
        out_specs=[vmem, far, far],
        scratch_shapes=scratch(blocks, own_cells, blocks, list_width, near_width)
        + [pltpu.VMEM(leaf.shape, leaf.dtype) for leaf in turned]
        + sums
        + [pltpu.SemaphoreType.DMA((2,))]
        + landing(numbers, [particles, tree_cells]),
        compiler_params=pltpu.CompilerParams(vmem_limit_bytes=127 * 2**19),
        cost_estimate=pl.CostEstimate(flops=10**9, bytes_accessed=10**6, transcendentals=10**6),
    )(*numbers, particles, tree_cells)

    return pl.pallas_call(
        functools.partial(moved_kernel, own_cells, near_slots),
        out_shape=jax.ShapeDtypeStruct(particles.shape, F32),
        in_specs=[far] * 7,
        out_specs=vmem,
        scratch_shapes=scratch(
            blocks, peers * slots, len(near_offsets) * near_slots, list_width, near_width
        )
        + sums
        + [pltpu.SMEM((own_cells + peers * slots,), jnp.int32)]
        + landing(numbers, [moved, particles, *turned, partial]),
        compiler_params=params,
    )(*numbers, moved, particles, *turned, partial)


def solution(mesh):
    return jax.shard_map(
        body,
        mesh=mesh,
        in_specs=(
            P(None, ("gx", "gy")),
            P(None, ("gx", "gy")),
            P(("gx", "gy"), None, None),
            P(("gx", "gy"), None),
            P(("gx", "gy"), None, None),
            P(("gx", "gy"), None),
            P(("gx", "gy"), None),
        ),
        out_specs=P(None, ("gx", "gy")),
        check_vma=False,
    )
```

```python
import functools

import jax
import jax.numpy as jnp
from jax import lax
from jax.experimental import pallas as pl
from jax.experimental.pallas import tpu as pltpu
from jax.sharding import PartitionSpec as P

BLK = 128
ROWS = 16
SUMS = 4
SOFTENING = 0.0025
near_offsets = (1, -1, 2, -2)
F32 = jnp.float32
B16 = jnp.bfloat16


def at_block(index):
    return pl.ds(pl.multiple_of(index * BLK, BLK), BLK)


def split3(value):
    high = value.astype(B16)
    rest = value - high.astype(F32)
    middle = rest.astype(B16)
    low = (rest - middle.astype(F32)).astype(B16)
    return high, middle, low


def split2(value):
    high = value.astype(B16)
    return high, (value - high.astype(F32)).astype(B16)


def stack_rows(rows):
    sub = lax.broadcasted_iota(jnp.int32, (8, BLK), 0)
    out = rows[0]
    for i in range(1, len(rows)):
        out = jnp.where(sub == i, rows[i], out)
    return out


def wide(row):
    return jnp.broadcast_to(row, (8, BLK))


def quadrupole_rows(x, y, z, xx, yy, xy, xz, yz):
    xx, yy, xy, xz, yz = (2.5 * v for v in (xx, yy, xy, xz, yz))
    zz = -(xx + yy)
    qx = xx * x + xy * y + xz * z
    qy = xy * x + yy * y + yz * z
    qz = xz * x + yz * y + zz * z
    inner = qx * x + qy * y + qz * z
    return [qx, qy, qz, inner, xx, yy, zz, xy, yz, xz]


def target_rows(x, y, z):
    one = jnp.ones((8, BLK), F32)
    first = stack_rows([-2 * x, -2 * y, -2 * z, one, x * x, y * y, z * z, 2 * x * y])
    second = stack_rows([2 * y * z, 2 * x * z] + [jnp.zeros((8, BLK), F32)] * 6)
    return jnp.concatenate([first, second], axis=0)


def six(weights):
    high, middle, low = weights[0:ROWS], weights[ROWS : 2 * ROWS], weights[2 * ROWS :]
    return jnp.concatenate([high, high, high, middle, middle, low], axis=0)


def contract(left, right):
    return lax.dot_general(left, right, (((1,), (1,)), ((), ())), preferred_element_type=F32)


def fetch(sources, targets, arrived):
    copies = [
        pltpu.make_async_copy(source, target, arrived.at[i])
        for i, (source, target) in enumerate(zip(sources, targets))
    ]
    for copy in copies:
        copy.start()
    return copies


def wait_for(copies):
    for copy in copies:
        copy.wait()


def pick_kernel(*refs):
    chosen_out = refs[5]
    chosen, sent, let_list, let_count, part_list, cells, particles, arrived = refs[6:]
    wait_for(fetch(refs[:5], refs[8:13], arrived))
    slots, peers = let_list.shape
    sub = lax.broadcasted_iota(jnp.int32, (4, BLK), 0)

    def peer_step(d, unused):
        count = let_count[0, d]
        for k in range(slots):
            columns = at_block(let_list[k, d])
            live = k < count
            chosen[d, k] = jnp.where(live, cells[0:4, columns], 0.0)
            quad = jnp.where(sub == 2, cells[8:9, columns], cells[4:8, columns])
            chosen[d, slots + k] = jnp.where(live, quad, 0.0)
            chosen[d, 2 * slots, k : k + 1, :] = jnp.where(live, cells[9:10, columns], 0.0)
        return unused

    for position, offset in enumerate(near_offsets):
        d = lax.axis_index(("gx", "gy")) + offset

        @pl.when((d >= 0) & (d < peers))
        def _():
            for k in range(part_list.shape[1]):
                chosen[d, 2 * slots + 1 + k] = particles[:, at_block(part_list[position, k])]

    chunks = sent.shape[0]
    copies = []
    for c in range(chunks):
        part = slice(c * peers // chunks, (c + 1) * peers // chunks)
        lax.fori_loop(part.start, part.stop, peer_step, 0, unroll=8)
        copies.append(pltpu.make_async_copy(chosen.at[part], chosen_out.at[part], sent.at[c]))
        copies[-1].start()
    wait_for(copies)


def put_eight(first, fields, rows):
    for i, value in enumerate(fields):
        rows[pl.ds(first * ROWS + i, 8, stride=ROWS), :] = value
    for i in range(len(fields), ROWS):
        rows[pl.ds(first * ROWS + i, 8, stride=ROWS), :] = jnp.zeros((8, BLK), F32)


def put_weights(b, rows, weights):
    high, middle, low = split3(rows[pl.ds(pl.multiple_of(b * ROWS, ROWS), ROWS), :])
    weights[b, 0:ROWS] = high
    weights[b, ROWS : 2 * ROWS] = middle
    weights[b, 2 * ROWS :] = low


def group(cells, near, j, first, near_first, lists, near_kept, targets, spread, places, weights,
          near_places, sums, quads):
    blocks = [lists[j, first + i] for i in range(cells)]
    near_blocks = [near_kept[j, near_first + i] for i in range(near)]
    if cells:
        coefficients = jnp.concatenate([six(weights[b]) for b in blocks], axis=1)
        bent = jnp.dot(targets[j], coefficients, preferred_element_type=F32)
    left = []
    for low in range(0, BLK, 16):
        rows = slice(low, low + 16)
        x, y, z = (spread[j, f, rows] for f in range(3))
        ax, ay, az, potential = (sums[j, f, rows] for f in range(SUMS))
        parts = []
        for i, (b, place) in enumerate(
            [(b, near_places) for b in near_blocks] + [(b, places) for b in blocks]
        ):
            rx, ry, rz = x - place[b, 0:1, :], y - place[b, 1:2, :], z - place[b, 2:3, :]
            inverse = lax.rsqrt(rx * rx + ry * ry + (rz * rz + SOFTENING))
            square = inverse * inverse
            pulled = inverse * place[b, 3:4, :]
            if i < near:
                radial = pulled * square
            else:
                fifth = square * square * inverse
                columns = slice((i - near) * BLK, (i - near + 1) * BLK)
                radial = square * (pulled + bent[rows, columns] * fifth)
                parts += split2(fifth)
            ax += radial * rx
            ay += radial * ry
            az += radial * rz
            potential += pulled
        for f, value in enumerate((ax, ay, az, potential)):
            sums[j, f, rows] = value
        if cells:
            left.append(jnp.concatenate(parts, axis=1))
    if cells:
        right = jnp.concatenate([weights[b] for b in blocks for _ in range(2)], axis=1)
        quads[j, :, : 3 * ROWS] += contract(jnp.concatenate(left, axis=0), right)


def add_block(j, count, near_count, list_next, *refs):
    fours = jnp.where(count >= 6, (count - 2) // 4, 0)
    fours = fours + (count - 4 * fours == 4).astype(jnp.int32)
    rest = count - 4 * fours

    def four(i, unused):
        group(4, 0, j, 4 * i, 0, *refs)
        return unused

    lax.fori_loop(0, fours, four, 0)
    for size, beside in ((1, 2), (2, 2), (3, 2), (5, 0)):

        @pl.when(rest == size)
        def _():
            group(size, beside, j, 4 * fours, 0, *refs)
            list_next()

    pl.when(rest == 0)(list_next)
    done = jnp.where((rest >= 1) & (rest <= 3), 2, 0)
    left = jnp.maximum(near_count - done, 0)
    near_fours = (left + 1) // 4

    def near_four(i, unused):
        group(0, 4, j, 0, done + 4 * i, *refs)
        return unused

    lax.fori_loop(0, near_fours, near_four, 0)

    @pl.when(4 * near_fours < left)
    def _():
        group(0, 2, j, 0, done + 4 * near_fours, *refs)


def keep_some(j, source, width, base, target, counts, live, nothing):
    count = jnp.int32(0)
    for l in range(width):
        index = source(j, l)
        target[j, count] = index - base
        count = count + live(index)
    for extra in range(3):
        target[j, count + extra] = nothing
    counts[j] = count


def selectors():
    shape = (ROWS, 7 * BLK)
    row = lax.broadcasted_iota(jnp.int32, shape, 0)
    lane = lax.broadcasted_iota(jnp.int32, shape, 1)
    inside = lane % BLK
    quad = (lane < 3 * BLK) & (inside < 3 * ROWS) & (inside % ROWS == row) & (row < 10)
    half = 2 * ((lane - 3 * BLK) // (2 * BLK)) + (inside >= BLK // 2).astype(jnp.int32)
    total = (lane >= 3 * BLK) & (half == row - (ROWS - SUMS))
    return jnp.where(quad | total, 1.0, 0.0).astype(B16)


def fold(first, second):
    low = lax.broadcasted_iota(jnp.int32, first.shape, 1) < BLK // 2
    return jnp.where(low, first, second) + pltpu.roll(jnp.where(low, second, first), BLK // 2, 1)


def forces_of(j, chooser, particles, sums, quads):
    parts = list(split3(quads[j]))
    for f in range(0, SUMS, 2):
        parts += split2(fold(sums[j, f], sums[j, f + 1]))
    mixed = contract(chooser, jnp.concatenate(parts, axis=1))
    qx, qy, qz, inner, xx, yy, zz, xy, yz, xz = (mixed[i : i + 1] for i in range(10))
    sx, sy, sz, pulls = (mixed[ROWS - SUMS + f : ROWS - SUMS + f + 1] for f in range(SUMS))
    x, y, z = (particles[f : f + 1, at_block(j)] for f in range(3))
    ax = xx * x + xy * y + xz * z
    ay = xy * x + yy * y + yz * z
    az = xz * x + yz * y + zz * z
    bent = ax * x + ay * y + az * z - 2 * (qx * x + qy * y + qz * z) + inner
    return (
        0.4 * (ax - qx) - sx,
        0.4 * (ay - qy) - sy,
        0.4 * (az - qz) - sz,
        -pulls - 0.2 * bent,
    )


def own_kernel(*refs):
    out, targets_out, spread_out = refs[4:7]
    (lists, list_counts, near_kept, near_counts, places, weights, near_places, fields, rows) = refs[7:16]
    targets, spread, sums, quads, sent, cell_lists, near_lists, particles, cells, arrived = refs[16:]
    copies = fetch(refs[:4], refs[21:25], arrived)
    blocks = cell_lists.shape[0]
    own_cells = cells.shape[1] // BLK
    clear(sums, quads)
    wait_for(copies)

    def by_field(b, unused):
        fields[pl.ds(b, 8, stride=own_cells), :] = cells[0:8, at_block(b)]
        fields[pl.ds(8 * own_cells + b, 2, stride=own_cells), :] = cells[8:10, at_block(b)]
        places[b] = cells[0:8, at_block(b)]
        return unused

    lax.fori_loop(0, own_cells, by_field, 0, unroll=16)

    def eight(g, unused):
        first = pl.multiple_of(8 * g, 8)
        x, y, z, _, xx, yy, _, xy, xz, yz = (
            fields[pl.ds(f * own_cells + first, 8), :] for f in range(10)
        )
        put_eight(first, quadrupole_rows(x, y, z, xx, yy, xy, xz, yz), rows)
        return unused

    lax.fori_loop(0, own_cells // 8, eight, 0, unroll=4)

    def step(b, unused):
        put_weights(b, rows, weights)
        return unused

    lax.fori_loop(0, own_cells, step, 0, unroll=16)
    weights[own_cells] = jnp.zeros((3 * ROWS, BLK), B16)
    places[own_cells] = jnp.zeros((8, BLK), F32)
    near_places[blocks] = jnp.zeros((8, BLK), F32)

    lane = lax.broadcasted_iota(jnp.int32, (BLK, BLK), 1)
    unit = jnp.where(lax.broadcasted_iota(jnp.int32, (BLK, BLK), 0) == lane, 1.0, 0.0).astype(B16)
    pick = coordinates()

    def prepare_target(j, unused):
        near_places[j, 0:4, :] = particles[:, at_block(j)]
        x, y, z = (wide(particles[f : f + 1, at_block(j)]) for f in range(3))
        high, middle, low = split3(target_rows(x, y, z))
        turned = contract(unit, jnp.concatenate([high, middle, low, high, middle, high], axis=0))
        turned = turned.astype(B16)
        targets[j] = turned
        begin_block(j, turned, pick, spread)
        return unused

    lax.fori_loop(0, blocks, prepare_target, 0, unroll=4)

    def make_lists(j):
        keep_some(
            j, lambda j, l: cell_lists[j, l], cell_lists.shape[1], 0, lists, list_counts,
            lambda b: (b < own_cells).astype(jnp.int32), own_cells,
        )
        keep_some(
            j, lambda j, l: near_lists[l, j], near_lists.shape[0], 0, near_kept, near_counts,
            lambda b: (b < blocks).astype(jnp.int32), blocks,
        )

    hand_on = fetch([targets, spread], [targets_out, spread_out], sent)
    add_all(
        blocks, make_lists, lists, list_counts, near_kept, near_counts, targets, spread, places, weights,
        near_places, sums, quads,
    )
    chooser = selectors()

    def finish_step(j, unused):
        for f, row in enumerate(forces_of(j, chooser, particles, sums, quads)):
            out[f : f + 1, at_block(j)] = row
        return unused

    lax.fori_loop(0, blocks, finish_step, 0, unroll=min(16, blocks))
    wait_for(hand_on)


def coordinates():
    shape = (6 * ROWS, 3 * BLK)
    row = lax.broadcasted_iota(jnp.int32, shape, 0)
    axis = lax.broadcasted_iota(jnp.int32, shape, 1) // BLK
    return jnp.where((row % ROWS == axis) & (row < 3 * ROWS), -0.5, 0.0).astype(B16)


def begin_block(j, turned, pick, spread):
    wider = jnp.dot(turned, pick, preferred_element_type=F32)
    for f in range(3):
        spread[j, f] = wider[:, f * BLK : (f + 1) * BLK]


def clear(sums, quads):
    def step(j, unused):
        for f in range(SUMS):
            sums[j, f] = jnp.zeros((BLK, BLK), F32)
        quads[j] = jnp.zeros((BLK, BLK), F32)
        return unused

    lax.fori_loop(0, quads.shape[0], step, 0)


def add_all(
    blocks, make_lists, lists, list_counts, near_kept, near_counts, targets, spread, places, weights,
    near_places, sums, quads,
):
    make_lists(0)

    def block_step(j, unused):
        add_block(
            j, list_counts[j], near_counts[j], lambda: make_lists(jnp.minimum(j + 1, blocks - 1)),
            lists, near_kept, targets, spread, places, weights, near_places, sums, quads,
        )
        return unused

    lax.fori_loop(0, blocks, block_step, 0)


def moved_kernel(own_cells, near_slots, *refs):
    out = refs[7]
    (lists, list_counts, near_kept, near_counts, places, weights, near_places, fields, rows) = refs[8:17]
    sums, quads, live = refs[17:20]
    cell_lists, near_lists, moved, particles, targets, spread, partial, arrived = refs[20:]
    copies = fetch(refs[:7], refs[20:27], arrived)
    blocks = cell_lists.shape[0]
    peers, slots = moved.shape[0], moved.shape[2]
    count = peers * slots
    near_moved = len(near_offsets) * near_slots
    me = lax.axis_index(("gx", "gy"))
    clear(sums, quads)

    def none_live(b, unused):
        live[b] = 0
        return unused

    lax.fori_loop(0, own_cells, none_live, 0, unroll=8)
    wait_for(copies[:3])

    def by_field(s, unused):
        for k in range(slots):
            b = s * slots + k
            fields[pl.ds(b, 4, stride=count), :] = moved[s, k]
            fields[pl.ds(4 * count + b, 4, stride=count), :] = moved[s, slots + k]
            places[b, 0:4, :] = moved[s, k]
        fields[pl.ds(8 * count + s * slots, slots), :] = moved[s, 2 * slots]
        return unused

    lax.fori_loop(0, peers, by_field, 0, unroll=8)

    bit = lax.broadcasted_iota(jnp.int32, (8, BLK), 0)

    def eight(g, unused):
        first = pl.multiple_of(8 * g, 8)
        x, y, z, mass, xx, yy, xz, xy, yz = (
            fields[pl.ds(f * count + first, 8), :] for f in range(9)
        )
        put_eight(first, quadrupole_rows(x, y, z, xx, yy, xy, xz, yz), rows)
        some = (mass != 0) | (xx != 0) | (yy != 0) | (xy != 0) | (xz != 0) | (yz != 0)
        some = jnp.max(jnp.where(some, 1.0, 0.0), axis=1, keepdims=True)
        code = jnp.sum(some * jnp.left_shift(1, bit[:, 0:1]).astype(F32)).astype(jnp.int32)
        for i in range(8):
            live[own_cells + first + i] = jnp.right_shift(code, i) & 1
        return unused

    lax.fori_loop(0, count // 8, eight, 0, unroll=8)
    weights[count] = jnp.zeros((3 * ROWS, BLK), B16)
    places[count] = jnp.zeros((8, BLK), F32)
    for position, offset in enumerate(near_offsets):
        source = me - offset
        there = (source >= 0) & (source < peers)
        safe = jnp.clip(source, 0, peers - 1)
        for k in range(near_slots):
            block = moved[safe, 2 * slots + 1 + k]
            near_places[position * near_slots + k, 0:4, :] = jnp.where(there, block, 0.0)
    near_places[near_moved] = jnp.zeros((8, BLK), F32)

    def step(b, unused):
        put_weights(b, rows, weights)
        return unused

    lax.fori_loop(0, count, step, 0, unroll=16)

    def make_lists(j):
        keep_some(
            j, lambda j, l: cell_lists[j, l], cell_lists.shape[1], own_cells, lists, list_counts,
            lambda b: live[b], count,
        )
        keep_some(
            j, lambda j, l: near_lists[l, j], near_lists.shape[0], blocks, near_kept, near_counts,
            lambda b: (b >= blocks).astype(jnp.int32), near_moved,
        )

    wait_for(copies[3:])
    add_all(
        blocks, make_lists, lists, list_counts, near_kept, near_counts, targets, spread, places, weights,
        near_places, sums, quads,
    )

    chooser = selectors()

    def finish_step(j, unused):
        for f, row in enumerate(forces_of(j, chooser, particles, sums, quads)):
            out[f : f + 1, at_block(j)] = row + partial[f : f + 1, at_block(j)]
        return unused

    lax.fori_loop(0, blocks, finish_step, 0, unroll=min(16, blocks))


def scratch(blocks, cells, near, list_width, near_width):
    return [
        pltpu.SMEM((blocks, list_width + 4), jnp.int32),
        pltpu.SMEM((blocks,), jnp.int32),
        pltpu.SMEM((blocks, near_width + 4), jnp.int32),
        pltpu.SMEM((blocks,), jnp.int32),
        pltpu.VMEM((cells + 1, 8, BLK), F32),
        pltpu.VMEM((cells + 1, 3 * ROWS, BLK), B16),
        pltpu.VMEM((near + 1, 8, BLK), F32),
        pltpu.VMEM((10 * cells, BLK), F32),
        pltpu.VMEM((ROWS * cells, BLK), F32),
    ]


def body(particles, tree_cells, let_list, let_count, part_list, cell_lists, near_lists):
    peers = lax.axis_size(("gx", "gy"))
    slots = let_list.shape[2]
    near_slots = part_list.shape[2]
    blocks, list_width = cell_lists.shape
    near_width = near_lists.shape[1]
    own_cells = tree_cells.shape[1] // BLK
    far = pl.BlockSpec(memory_space=pltpu.HBM)
    vmem = pl.BlockSpec(memory_space=pltpu.VMEM)
    params = pltpu.CompilerParams(vmem_limit_bytes=60 * 2**20)

    def landing(numbers, arrays):
        spaces = [pltpu.SMEM(a.shape, a.dtype) for a in numbers]
        spaces += [pltpu.VMEM(a.shape, a.dtype) for a in arrays]
        return spaces + [pltpu.SemaphoreType.DMA((len(spaces),))]

    choice = [jnp.transpose(let_list[0]), let_count, part_list[0]]
    chosen = pl.pallas_call(
        pick_kernel,
        out_shape=jax.ShapeDtypeStruct((peers, 2 * slots + 1 + near_slots, 4, BLK), F32),
        in_specs=[far] * 5,
        out_specs=far,
        scratch_shapes=[
            pltpu.VMEM((peers, 2 * slots + 1 + near_slots, 4, BLK), F32),
            pltpu.SemaphoreType.DMA((4,)),
        ]
        + landing(choice, [tree_cells, particles]),
        compiler_params=params,
    )(*choice, tree_cells, particles)
    moved = lax.all_to_all(chosen, ("gx", "gy"), split_axis=0, concat_axis=0, tiled=True)

    numbers = [cell_lists, jnp.transpose(near_lists)]
    turned = [
        jax.ShapeDtypeStruct((blocks, BLK, 6 * ROWS), B16),
        jax.ShapeDtypeStruct((blocks, 3, BLK, BLK), F32),
    ]
    sums = [pltpu.VMEM((blocks, SUMS, BLK, BLK), F32), pltpu.VMEM((blocks, BLK, BLK), F32)]
    partial, *turned = pl.pallas_call(
        own_kernel,
        out_shape=[jax.ShapeDtypeStruct(particles.shape, F32)] + turned,
        in_specs=[far] * 4,
        out_specs=[vmem, far, far],
        scratch_shapes=scratch(blocks, own_cells, blocks, list_width, near_width)
        + [pltpu.VMEM(leaf.shape, leaf.dtype) for leaf in turned]
        + sums
        + [pltpu.SemaphoreType.DMA((2,))]
        + landing(numbers, [particles, tree_cells]),
        compiler_params=pltpu.CompilerParams(vmem_limit_bytes=127 * 2**19),
        cost_estimate=pl.CostEstimate(flops=10**9, bytes_accessed=10**6, transcendentals=10**6),
    )(*numbers, particles, tree_cells)

    return pl.pallas_call(
        functools.partial(moved_kernel, own_cells, near_slots),
        out_shape=jax.ShapeDtypeStruct(particles.shape, F32),
        in_specs=[far] * 7,
        out_specs=vmem,
        scratch_shapes=scratch(
            blocks, peers * slots, len(near_offsets) * near_slots, list_width, near_width
        )
        + sums
        + [pltpu.SMEM((own_cells + peers * slots,), jnp.int32)]
        + landing(numbers, [moved, particles, *turned, partial]),
        compiler_params=params,
    )(*numbers, moved, particles, *turned, partial)


def solution(mesh):
    return jax.shard_map(
        body,
        mesh=mesh,
        in_specs=(
            P(None, ("gx", "gy")),
            P(None, ("gx", "gy")),
            P(("gx", "gy"), None, None),
            P(("gx", "gy"), None),
            P(("gx", "gy"), None, None),
            P(("gx", "gy"), None),
            P(("gx", "gy"), None),
        ),
        out_specs=P(None, ("gx", "gy")),
        check_vma=False,
    )
```

```python
import functools

import jax
import jax.numpy as jnp
from jax import lax
from jax.experimental import pallas as pl
from jax.experimental.pallas import tpu as pltpu
from jax.sharding import PartitionSpec as P

BLK = 128
ROWS = 16
SUMS = 4
SOFTENING = 0.0025
near_offsets = (1, -1, 2, -2)
F32 = jnp.float32
B16 = jnp.bfloat16


def at_block(index):
    return pl.ds(pl.multiple_of(index * BLK, BLK), BLK)


def split3(value):
    high = value.astype(B16)
    rest = value - high.astype(F32)
    middle = rest.astype(B16)
    low = (rest - middle.astype(F32)).astype(B16)
    return high, middle, low


def split2(value):
    high = value.astype(B16)
    return high, (value - high.astype(F32)).astype(B16)


def stack_rows(rows):
    sub = lax.broadcasted_iota(jnp.int32, (8, BLK), 0)
    out = rows[0]
    for i in range(1, len(rows)):
        out = jnp.where(sub == i, rows[i], out)
    return out


def wide(row):
    return jnp.broadcast_to(row, (8, BLK))


def quadrupole_rows(x, y, z, xx, yy, xy, xz, yz):
    xx, yy, xy, xz, yz = (2.5 * v for v in (xx, yy, xy, xz, yz))
    zz = -(xx + yy)
    qx = xx * x + xy * y + xz * z
    qy = xy * x + yy * y + yz * z
    qz = xz * x + yz * y + zz * z
    inner = qx * x + qy * y + qz * z
    return [qx, qy, qz, inner, xx, yy, zz, xy, yz, xz]


def target_rows(x, y, z):
    one = jnp.ones((8, BLK), F32)
    first = stack_rows([-2 * x, -2 * y, -2 * z, one, x * x, y * y, z * z, 2 * x * y])
    second = stack_rows([2 * y * z, 2 * x * z] + [jnp.zeros((8, BLK), F32)] * 6)
    return jnp.concatenate([first, second], axis=0)


def six(weights):
    high, middle, low = weights[0:ROWS], weights[ROWS : 2 * ROWS], weights[2 * ROWS :]
    return jnp.concatenate([high, high, high, middle, middle, low], axis=0)


def contract(left, right):
    return lax.dot_general(left, right, (((1,), (1,)), ((), ())), preferred_element_type=F32)


def fetch(sources, targets, arrived):
    copies = [
        pltpu.make_async_copy(source, target, arrived.at[i])
        for i, (source, target) in enumerate(zip(sources, targets))
    ]
    for copy in copies:
        copy.start()
    return copies


def wait_for(copies):
    for copy in copies:
        copy.wait()


def pick_kernel(*refs):
    chosen_out = refs[5]
    chosen, sent, let_list, let_count, part_list, cells, particles, arrived = refs[6:]
    wait_for(fetch(refs[:5], refs[8:13], arrived))
    slots, peers = let_list.shape
    sub = lax.broadcasted_iota(jnp.int32, (4, BLK), 0)

    def peer_step(d, unused):
        count = let_count[0, d]
        for k in range(slots):
            columns = at_block(let_list[k, d])
            live = k < count
            chosen[d, k] = jnp.where(live, cells[0:4, columns], 0.0)
            quad = jnp.where(sub == 2, cells[8:9, columns], cells[4:8, columns])
            chosen[d, slots + k] = jnp.where(live, quad, 0.0)
            chosen[d, 2 * slots, k : k + 1, :] = jnp.where(live, cells[9:10, columns], 0.0)
        return unused

    for position, offset in enumerate(near_offsets):
        d = lax.axis_index(("gx", "gy")) + offset

        @pl.when((d >= 0) & (d < peers))
        def _():
            for k in range(part_list.shape[1]):
                chosen[d, 2 * slots + 1 + k] = particles[:, at_block(part_list[position, k])]

    chunks = sent.shape[0]
    copies = []
    for c in range(chunks):
        part = slice(c * peers // chunks, (c + 1) * peers // chunks)
        lax.fori_loop(part.start, part.stop, peer_step, 0, unroll=8)
        copies.append(pltpu.make_async_copy(chosen.at[part], chosen_out.at[part], sent.at[c]))
        copies[-1].start()
    wait_for(copies)


def put_eight(first, fields, rows):
    for i, value in enumerate(fields):
        rows[pl.ds(first * ROWS + i, 8, stride=ROWS), :] = value
    for i in range(len(fields), ROWS):
        rows[pl.ds(first * ROWS + i, 8, stride=ROWS), :] = jnp.zeros((8, BLK), F32)


def put_weights(b, rows, weights):
    high, middle, low = split3(rows[pl.ds(pl.multiple_of(b * ROWS, ROWS), ROWS), :])
    weights[b, 0:ROWS] = high
    weights[b, ROWS : 2 * ROWS] = middle
    weights[b, 2 * ROWS :] = low


def group(cells, near, j, first, near_first, lists, near_kept, targets, spread, places, weights,
          near_places, sums, quads):
    blocks = [lists[j, first + i] for i in range(cells)]
    near_blocks = [near_kept[j, near_first + i] for i in range(near)]
    if cells:
        coefficients = jnp.concatenate([six(weights[b]) for b in blocks], axis=1)
        bent = jnp.dot(targets[j], coefficients, preferred_element_type=F32)
    left = []
    for low in range(0, BLK, 16):
        rows = slice(low, low + 16)
        x, y, z = (spread[j, f, rows] for f in range(3))
        ax, ay, az, potential = (sums[j, f, rows] for f in range(SUMS))
        parts = []
        for i, (b, place) in enumerate(
            [(b, near_places) for b in near_blocks] + [(b, places) for b in blocks]
        ):
            rx, ry, rz = x - place[b, 0:1, :], y - place[b, 1:2, :], z - place[b, 2:3, :]
            inverse = lax.rsqrt(rx * rx + ry * ry + (rz * rz + SOFTENING))
            square = inverse * inverse
            pulled = inverse * place[b, 3:4, :]
            if i < near:
                radial = pulled * square
            else:
                fifth = square * square * inverse
                columns = slice((i - near) * BLK, (i - near + 1) * BLK)
                radial = square * (pulled + bent[rows, columns] * fifth)
                parts += split2(fifth)
            ax += radial * rx
            ay += radial * ry
            az += radial * rz
            potential += pulled
        for f, value in enumerate((ax, ay, az, potential)):
            sums[j, f, rows] = value
        if cells:
            left.append(jnp.concatenate(parts, axis=1))
    if cells:
        right = jnp.concatenate([weights[b] for b in blocks for _ in range(2)], axis=1)
        quads[j, :, : 3 * ROWS] += contract(jnp.concatenate(left, axis=0), right)


def add_block(j, count, near_count, list_next, *refs):
    fours = jnp.where(count >= 6, (count - 2) // 4, 0)
    rest = count - 4 * fours

    def four(i, unused):
        group(4, 0, j, 4 * i, 0, *refs)
        return unused

    lax.fori_loop(0, fours, four, 0)
    for size, beside in ((1, 2), (2, 2), (3, 2), (4, 2), (5, 2)):

        @pl.when(rest == size)
        def _():
            group(size, beside, j, 4 * fours, 0, *refs)
            list_next()

    pl.when(rest == 0)(list_next)
    done = jnp.where(rest > 0, 2, 0)
    left = jnp.maximum(near_count - done, 0)
    near_fours = left // 4

    def near_four(i, unused):
        group(0, 4, j, 0, done + 4 * i, *refs)
        return unused

    lax.fori_loop(0, near_fours, near_four, 0)
    for size in (1, 2, 3):

        @pl.when(left - 4 * near_fours == size)
        def _():
            group(0, size, j, 0, done + 4 * near_fours, *refs)


def keep_some(j, source, width, base, target, counts, live, nothing):
    count = jnp.int32(0)
    for l in range(width):
        index = source(j, l)
        target[j, count] = index - base
        count = count + live(index)
    for extra in range(3):
        target[j, count + extra] = nothing
    counts[j] = count


def selectors():
    shape = (ROWS, 7 * BLK)
    row = lax.broadcasted_iota(jnp.int32, shape, 0)
    lane = lax.broadcasted_iota(jnp.int32, shape, 1)
    inside = lane % BLK
    quad = (lane < 3 * BLK) & (inside < 3 * ROWS) & (inside % ROWS == row) & (row < 10)
    half = 2 * ((lane - 3 * BLK) // (2 * BLK)) + (inside >= BLK // 2).astype(jnp.int32)
    total = (lane >= 3 * BLK) & (half == row - (ROWS - SUMS))
    return jnp.where(quad | total, 1.0, 0.0).astype(B16)


def fold(first, second):
    low = lax.broadcasted_iota(jnp.int32, first.shape, 1) < BLK // 2
    return jnp.where(low, first, second) + pltpu.roll(jnp.where(low, second, first), BLK // 2, 1)


def forces_of(j, chooser, particles, sums, quads):
    parts = list(split3(quads[j]))
    for f in range(0, SUMS, 2):
        parts += split2(fold(sums[j, f], sums[j, f + 1]))
    mixed = contract(chooser, jnp.concatenate(parts, axis=1))
    qx, qy, qz, inner, xx, yy, zz, xy, yz, xz = (mixed[i : i + 1] for i in range(10))
    sx, sy, sz, pulls = (mixed[ROWS - SUMS + f : ROWS - SUMS + f + 1] for f in range(SUMS))
    x, y, z = (particles[f : f + 1, at_block(j)] for f in range(3))
    ax = xx * x + xy * y + xz * z
    ay = xy * x + yy * y + yz * z
    az = xz * x + yz * y + zz * z
    bent = ax * x + ay * y + az * z - 2 * (qx * x + qy * y + qz * z) + inner
    return (
        0.4 * (ax - qx) - sx,
        0.4 * (ay - qy) - sy,
        0.4 * (az - qz) - sz,
        -pulls - 0.2 * bent,
    )


def own_kernel(*refs):
    out, targets_out, spread_out = refs[4:7]
    (lists, list_counts, near_kept, near_counts, places, weights, near_places, fields, rows) = refs[7:16]
    targets, spread, sums, quads, sent, cell_lists, near_lists, particles, cells, arrived = refs[16:]
    copies = fetch(refs[:4], refs[21:25], arrived)
    blocks = cell_lists.shape[0]
    own_cells = cells.shape[1] // BLK
    clear(sums, quads)
    wait_for(copies)

    def by_field(b, unused):
        fields[pl.ds(b, 8, stride=own_cells), :] = cells[0:8, at_block(b)]
        fields[pl.ds(8 * own_cells + b, 2, stride=own_cells), :] = cells[8:10, at_block(b)]
        places[b] = cells[0:8, at_block(b)]
        return unused

    lax.fori_loop(0, own_cells, by_field, 0, unroll=16)

    def eight(g, unused):
        first = pl.multiple_of(8 * g, 8)
        x, y, z, _, xx, yy, _, xy, xz, yz = (
            fields[pl.ds(f * own_cells + first, 8), :] for f in range(10)
        )
        put_eight(first, quadrupole_rows(x, y, z, xx, yy, xy, xz, yz), rows)
        return unused

    lax.fori_loop(0, own_cells // 8, eight, 0, unroll=4)

    def step(b, unused):
        put_weights(b, rows, weights)
        return unused

    lax.fori_loop(0, own_cells, step, 0, unroll=16)
    weights[own_cells] = jnp.zeros((3 * ROWS, BLK), B16)
    places[own_cells] = jnp.zeros((8, BLK), F32)
    near_places[blocks] = jnp.zeros((8, BLK), F32)

    lane = lax.broadcasted_iota(jnp.int32, (BLK, BLK), 1)
    unit = jnp.where(lax.broadcasted_iota(jnp.int32, (BLK, BLK), 0) == lane, 1.0, 0.0).astype(B16)
    pick = coordinates()

    def prepare_target(j, unused):
        near_places[j, 0:4, :] = particles[:, at_block(j)]
        x, y, z = (wide(particles[f : f + 1, at_block(j)]) for f in range(3))
        high, middle, low = split3(target_rows(x, y, z))
        turned = contract(unit, jnp.concatenate([high, middle, low, high, middle, high], axis=0))
        turned = turned.astype(B16)
        targets[j] = turned
        begin_block(j, turned, pick, spread)
        return unused

    lax.fori_loop(0, blocks, prepare_target, 0, unroll=4)

    def make_lists(j):
        keep_some(
            j, lambda j, l: cell_lists[j, l], cell_lists.shape[1], 0, lists, list_counts,
            lambda b: (b < own_cells).astype(jnp.int32), own_cells,
        )
        keep_some(
            j, lambda j, l: near_lists[l, j], near_lists.shape[0], 0, near_kept, near_counts,
            lambda b: (b < blocks).astype(jnp.int32), blocks,
        )

    hand_on = fetch([targets, spread], [targets_out, spread_out], sent)
    add_all(
        blocks, make_lists, lists, list_counts, near_kept, near_counts, targets, spread, places, weights,
        near_places, sums, quads,
    )
    chooser = selectors()

    def finish_step(j, unused):
        for f, row in enumerate(forces_of(j, chooser, particles, sums, quads)):
            out[f : f + 1, at_block(j)] = row
        return unused

    lax.fori_loop(0, blocks, finish_step, 0, unroll=min(16, blocks))
    wait_for(hand_on)


def coordinates():
    shape = (6 * ROWS, 3 * BLK)
    row = lax.broadcasted_iota(jnp.int32, shape, 0)
    axis = lax.broadcasted_iota(jnp.int32, shape, 1) // BLK
    return jnp.where((row % ROWS == axis) & (row < 3 * ROWS), -0.5, 0.0).astype(B16)


def begin_block(j, turned, pick, spread):
    wider = jnp.dot(turned, pick, preferred_element_type=F32)
    for f in range(3):
        spread[j, f] = wider[:, f * BLK : (f + 1) * BLK]


def clear(sums, quads):
    def step(j, unused):
        for f in range(SUMS):
            sums[j, f] = jnp.zeros((BLK, BLK), F32)
        quads[j] = jnp.zeros((BLK, BLK), F32)
        return unused

    lax.fori_loop(0, quads.shape[0], step, 0)


def add_all(
    blocks, make_lists, lists, list_counts, near_kept, near_counts, targets, spread, places, weights,
    near_places, sums, quads,
):
    make_lists(0)

    def block_step(j, unused):
        add_block(
            j, list_counts[j], near_counts[j], lambda: make_lists(jnp.minimum(j + 1, blocks - 1)),
            lists, near_kept, targets, spread, places, weights, near_places, sums, quads,
        )
        return unused

    lax.fori_loop(0, blocks, block_step, 0)


def moved_kernel(own_cells, near_slots, *refs):
    out = refs[7]
    (lists, list_counts, near_kept, near_counts, places, weights, near_places, fields, rows) = refs[8:17]
    sums, quads, live = refs[17:20]
    cell_lists, near_lists, moved, particles, targets, spread, partial, arrived = refs[20:]
    copies = fetch(refs[:7], refs[20:27], arrived)
    blocks = cell_lists.shape[0]
    peers, slots = moved.shape[0], moved.shape[2]
    count = peers * slots
    near_moved = len(near_offsets) * near_slots
    me = lax.axis_index(("gx", "gy"))
    clear(sums, quads)

    def none_live(b, unused):
        live[b] = 0
        return unused

    lax.fori_loop(0, own_cells, none_live, 0, unroll=8)
    wait_for(copies[:3])

    def by_field(s, unused):
        for k in range(slots):
            b = s * slots + k
            fields[pl.ds(b, 4, stride=count), :] = moved[s, k]
            fields[pl.ds(4 * count + b, 4, stride=count), :] = moved[s, slots + k]
            places[b, 0:4, :] = moved[s, k]
        fields[pl.ds(8 * count + s * slots, slots), :] = moved[s, 2 * slots]
        return unused

    lax.fori_loop(0, peers, by_field, 0, unroll=8)

    bit = lax.broadcasted_iota(jnp.int32, (8, BLK), 0)

    def eight(g, unused):
        first = pl.multiple_of(8 * g, 8)
        x, y, z, mass, xx, yy, xz, xy, yz = (
            fields[pl.ds(f * count + first, 8), :] for f in range(9)
        )
        put_eight(first, quadrupole_rows(x, y, z, xx, yy, xy, xz, yz), rows)
        some = (mass != 0) | (xx != 0) | (yy != 0) | (xy != 0) | (xz != 0) | (yz != 0)
        some = jnp.max(jnp.where(some, 1.0, 0.0), axis=1, keepdims=True)
        code = jnp.sum(some * jnp.left_shift(1, bit[:, 0:1]).astype(F32)).astype(jnp.int32)
        for i in range(8):
            live[own_cells + first + i] = jnp.right_shift(code, i) & 1
        return unused

    lax.fori_loop(0, count // 8, eight, 0, unroll=8)
    weights[count] = jnp.zeros((3 * ROWS, BLK), B16)
    places[count] = jnp.zeros((8, BLK), F32)
    for position, offset in enumerate(near_offsets):
        source = me - offset
        there = (source >= 0) & (source < peers)
        safe = jnp.clip(source, 0, peers - 1)
        for k in range(near_slots):
            block = moved[safe, 2 * slots + 1 + k]
            near_places[position * near_slots + k, 0:4, :] = jnp.where(there, block, 0.0)
    near_places[near_moved] = jnp.zeros((8, BLK), F32)

    def step(b, unused):
        put_weights(b, rows, weights)
        return unused

    lax.fori_loop(0, count, step, 0, unroll=16)

    def make_lists(j):
        keep_some(
            j, lambda j, l: cell_lists[j, l], cell_lists.shape[1], own_cells, lists, list_counts,
            lambda b: live[b], count,
        )
        keep_some(
            j, lambda j, l: near_lists[l, j], near_lists.shape[0], blocks, near_kept, near_counts,
            lambda b: (b >= blocks).astype(jnp.int32), near_moved,
        )

    wait_for(copies[3:])
    add_all(
        blocks, make_lists, lists, list_counts, near_kept, near_counts, targets, spread, places, weights,
        near_places, sums, quads,
    )

    chooser = selectors()

    def finish_step(j, unused):
        for f, row in enumerate(forces_of(j, chooser, particles, sums, quads)):
            out[f : f + 1, at_block(j)] = row + partial[f : f + 1, at_block(j)]
        return unused

    lax.fori_loop(0, blocks, finish_step, 0, unroll=min(16, blocks))


def scratch(blocks, cells, near, list_width, near_width):
    return [
        pltpu.SMEM((blocks, list_width + 4), jnp.int32),
        pltpu.SMEM((blocks,), jnp.int32),
        pltpu.SMEM((blocks, near_width + 4), jnp.int32),
        pltpu.SMEM((blocks,), jnp.int32),
        pltpu.VMEM((cells + 1, 8, BLK), F32),
        pltpu.VMEM((cells + 1, 3 * ROWS, BLK), B16),
        pltpu.VMEM((near + 1, 8, BLK), F32),
        pltpu.VMEM((10 * cells, BLK), F32),
        pltpu.VMEM((ROWS * cells, BLK), F32),
    ]


def body(particles, tree_cells, let_list, let_count, part_list, cell_lists, near_lists):
    peers = lax.axis_size(("gx", "gy"))
    slots = let_list.shape[2]
    near_slots = part_list.shape[2]
    blocks, list_width = cell_lists.shape
    near_width = near_lists.shape[1]
    own_cells = tree_cells.shape[1] // BLK
    far = pl.BlockSpec(memory_space=pltpu.HBM)
    vmem = pl.BlockSpec(memory_space=pltpu.VMEM)
    params = pltpu.CompilerParams(vmem_limit_bytes=60 * 2**20)

    def landing(numbers, arrays):
        spaces = [pltpu.SMEM(a.shape, a.dtype) for a in numbers]
        spaces += [pltpu.VMEM(a.shape, a.dtype) for a in arrays]
        return spaces + [pltpu.SemaphoreType.DMA((len(spaces),))]

    choice = [jnp.transpose(let_list[0]), let_count, part_list[0]]
    chosen = pl.pallas_call(
        pick_kernel,
        out_shape=jax.ShapeDtypeStruct((peers, 2 * slots + 1 + near_slots, 4, BLK), F32),
        in_specs=[far] * 5,
        out_specs=far,
        scratch_shapes=[
            pltpu.VMEM((peers, 2 * slots + 1 + near_slots, 4, BLK), F32),
            pltpu.SemaphoreType.DMA((4,)),
        ]
        + landing(choice, [tree_cells, particles]),
        compiler_params=params,
    )(*choice, tree_cells, particles)
    moved = lax.all_to_all(chosen, ("gx", "gy"), split_axis=0, concat_axis=0, tiled=True)

    numbers = [cell_lists, jnp.transpose(near_lists)]
    turned = [
        jax.ShapeDtypeStruct((blocks, BLK, 6 * ROWS), B16),
        jax.ShapeDtypeStruct((blocks, 3, BLK, BLK), F32),
    ]
    sums = [pltpu.VMEM((blocks, SUMS, BLK, BLK), F32), pltpu.VMEM((blocks, BLK, BLK), F32)]
    partial, *turned = pl.pallas_call(
        own_kernel,
        out_shape=[jax.ShapeDtypeStruct(particles.shape, F32)] + turned,
        in_specs=[far] * 4,
        out_specs=[vmem, far, far],
        scratch_shapes=scratch(blocks, own_cells, blocks, list_width, near_width)
        + [pltpu.VMEM(leaf.shape, leaf.dtype) for leaf in turned]
        + sums
        + [pltpu.SemaphoreType.DMA((2,))]
        + landing(numbers, [particles, tree_cells]),
        compiler_params=pltpu.CompilerParams(vmem_limit_bytes=127 * 2**19),
        cost_estimate=pl.CostEstimate(flops=10**9, bytes_accessed=10**6, transcendentals=10**6),
    )(*numbers, particles, tree_cells)

    return pl.pallas_call(
        functools.partial(moved_kernel, own_cells, near_slots),
        out_shape=jax.ShapeDtypeStruct(particles.shape, F32),
        in_specs=[far] * 7,
        out_specs=vmem,
        scratch_shapes=scratch(
            blocks, peers * slots, len(near_offsets) * near_slots, list_width, near_width
        )
        + sums
        + [pltpu.SMEM((own_cells + peers * slots,), jnp.int32)]
        + landing(numbers, [moved, particles, *turned, partial]),
        compiler_params=params,
    )(*numbers, moved, particles, *turned, partial)


def solution(mesh):
    return jax.shard_map(
        body,
        mesh=mesh,
        in_specs=(
            P(None, ("gx", "gy")),
            P(None, ("gx", "gy")),
            P(("gx", "gy"), None, None),
            P(("gx", "gy"), None),
            P(("gx", "gy"), None, None),
            P(("gx", "gy"), None),
            P(("gx", "gy"), None),
        ),
        out_specs=P(None, ("gx", "gy")),
        check_vma=False,
    )
```

```python
import functools

import jax
import jax.numpy as jnp
from jax import lax
from jax.experimental import pallas as pl
from jax.experimental.pallas import tpu as pltpu
from jax.sharding import PartitionSpec as P

BLK = 128
ROWS = 16
SUMS = 4
SOFTENING = 0.0025
near_offsets = (1, -1, 2, -2)
F32 = jnp.float32
B16 = jnp.bfloat16


def at_block(index):
    return pl.ds(pl.multiple_of(index * BLK, BLK), BLK)


def split3(value):
    high = value.astype(B16)
    rest = value - high.astype(F32)
    middle = rest.astype(B16)
    low = (rest - middle.astype(F32)).astype(B16)
    return high, middle, low


def split2(value):
    high = value.astype(B16)
    return high, (value - high.astype(F32)).astype(B16)


def stack_rows(rows):
    sub = lax.broadcasted_iota(jnp.int32, (8, BLK), 0)
    out = rows[0]
    for i in range(1, len(rows)):
        out = jnp.where(sub == i, rows[i], out)
    return out


def wide(row):
    return jnp.broadcast_to(row, (8, BLK))


def quadrupole_rows(x, y, z, xx, yy, xy, xz, yz):
    xx, yy, xy, xz, yz = (2.5 * v for v in (xx, yy, xy, xz, yz))
    zz = -(xx + yy)
    qx = xx * x + xy * y + xz * z
    qy = xy * x + yy * y + yz * z
    qz = xz * x + yz * y + zz * z
    inner = qx * x + qy * y + qz * z
    return [qx, qy, qz, inner, xx, yy, zz, xy, yz, xz]


def target_rows(x, y, z):
    one = jnp.ones((8, BLK), F32)
    first = stack_rows([-2 * x, -2 * y, -2 * z, one, x * x, y * y, z * z, 2 * x * y])
    second = stack_rows([2 * y * z, 2 * x * z] + [jnp.zeros((8, BLK), F32)] * 6)
    return jnp.concatenate([first, second], axis=0)


def six(weights):
    high, middle, low = weights[0:ROWS], weights[ROWS : 2 * ROWS], weights[2 * ROWS :]
    return jnp.concatenate([high, high, high, middle, middle, low], axis=0)


def contract(left, right):
    return lax.dot_general(left, right, (((1,), (1,)), ((), ())), preferred_element_type=F32)


def fetch(sources, targets, arrived):
    copies = [
        pltpu.make_async_copy(source, target, arrived.at[i])
        for i, (source, target) in enumerate(zip(sources, targets))
    ]
    for copy in copies:
        copy.start()
    return copies


def wait_for(copies):
    for copy in copies:
        copy.wait()


def pick_kernel(*refs):
    chosen_out = refs[5]
    chosen, sent, let_list, let_count, part_list, cells, particles, arrived = refs[6:]
    wait_for(fetch(refs[:5], refs[8:13], arrived))
    slots, peers = let_list.shape
    sub = lax.broadcasted_iota(jnp.int32, (4, BLK), 0)

    def peer_step(d, unused):
        count = let_count[0, d]
        for k in range(slots):
            columns = at_block(let_list[k, d])
            live = k < count
            chosen[d, k] = jnp.where(live, cells[0:4, columns], 0.0)
            quad = jnp.where(sub == 2, cells[8:9, columns], cells[4:8, columns])
            chosen[d, slots + k] = jnp.where(live, quad, 0.0)
            chosen[d, 2 * slots, k : k + 1, :] = jnp.where(live, cells[9:10, columns], 0.0)
        return unused

    for position, offset in enumerate(near_offsets):
        d = lax.axis_index(("gx", "gy")) + offset

        @pl.when((d >= 0) & (d < peers))
        def _():
            for k in range(part_list.shape[1]):
                chosen[d, 2 * slots + 1 + k] = particles[:, at_block(part_list[position, k])]

    chunks = sent.shape[0]
    copies = []
    for c in range(chunks):
        part = slice(c * peers // chunks, (c + 1) * peers // chunks)
        lax.fori_loop(part.start, part.stop, peer_step, 0, unroll=8)
        copies.append(pltpu.make_async_copy(chosen.at[part], chosen_out.at[part], sent.at[c]))
        copies[-1].start()
    wait_for(copies)


def put_eight(first, fields, rows):
    for i, value in enumerate(fields):
        rows[pl.ds(first * ROWS + i, 8, stride=ROWS), :] = value
    for i in range(len(fields), ROWS):
        rows[pl.ds(first * ROWS + i, 8, stride=ROWS), :] = jnp.zeros((8, BLK), F32)


def put_weights(b, rows, weights):
    high, middle, low = split3(rows[pl.ds(pl.multiple_of(b * ROWS, ROWS), ROWS), :])
    weights[b, 0:ROWS] = high
    weights[b, ROWS : 2 * ROWS] = middle
    weights[b, 2 * ROWS :] = low


def group(cells, near, j, first, near_first, lists, near_kept, targets, spread, places, weights,
          near_places, sums, quads):
    blocks = [lists[j, first + i] for i in range(cells)]
    near_blocks = [near_kept[j, near_first + i] for i in range(near)]
    if cells:
        coefficients = jnp.concatenate([six(weights[b]) for b in blocks], axis=1)
        bent = jnp.dot(targets[j], coefficients, preferred_element_type=F32)
    left = []
    for low in range(0, BLK, 16):
        rows = slice(low, low + 16)
        x, y, z = (spread[j, f, rows] for f in range(3))
        ax, ay, az, potential = (sums[j, f, rows] for f in range(SUMS))
        parts = []
        for i, (b, place) in enumerate(
            [(b, near_places) for b in near_blocks] + [(b, places) for b in blocks]
        ):
            rx, ry, rz = x - place[b, 0:1, :], y - place[b, 1:2, :], z - place[b, 2:3, :]
            inverse = lax.rsqrt(rx * rx + ry * ry + (rz * rz + SOFTENING))
            square = inverse * inverse
            pulled = inverse * place[b, 3:4, :]
            if i < near:
                radial = pulled * square
            else:
                fifth = square * square * inverse
                columns = slice((i - near) * BLK, (i - near + 1) * BLK)
                radial = square * (pulled + bent[rows, columns] * fifth)
                parts += split2(fifth)
            ax += radial * rx
            ay += radial * ry
            az += radial * rz
            potential += pulled
        for f, value in enumerate((ax, ay, az, potential)):
            sums[j, f, rows] = value
        if cells:
            left.append(jnp.concatenate(parts, axis=1))
    if cells:
        right = jnp.concatenate([weights[b] for b in blocks for _ in range(2)], axis=1)
        quads[j, :, : 3 * ROWS] += contract(jnp.concatenate(left, axis=0), right)


def add_block(j, count, near_count, list_next, *refs):
    fours = jnp.where(count >= 6, (count - 2) // 4, 0)
    rest = count - 4 * fours

    def four(i, unused):
        group(4, 0, j, 4 * i, 0, *refs)
        return unused

    lax.fori_loop(0, fours, four, 0)
    for size, beside in ((1, 2), (2, 2), (3, 2), (4, 2), (5, 2)):

        @pl.when(rest == size)
        def _():
            group(size, beside, j, 4 * fours, 0, *refs)
            list_next()

    pl.when(rest == 0)(list_next)
    done = jnp.where(rest > 0, 2, 0)
    left = jnp.maximum(near_count - done, 0)
    near_fours = left // 4

    def near_four(i, unused):
        group(0, 4, j, 0, done + 4 * i, *refs)
        return unused

    lax.fori_loop(0, near_fours, near_four, 0)
    for size in (1, 2, 3):

        @pl.when(left - 4 * near_fours == size)
        def _():
            group(0, size, j, 0, done + 4 * near_fours, *refs)


def keep_some(j, source, width, base, target, counts, live, nothing):
    count = jnp.int32(0)
    for l in range(width):
        index = source(j, l)
        target[j, count] = index - base
        count = count + live(index)
    for extra in range(3):
        target[j, count + extra] = nothing
    counts[j] = count


def selectors():
    shape = (ROWS, 7 * BLK)
    row = lax.broadcasted_iota(jnp.int32, shape, 0)
    lane = lax.broadcasted_iota(jnp.int32, shape, 1)
    inside = lane % BLK
    quad = (lane < 3 * BLK) & (inside < 3 * ROWS) & (inside % ROWS == row) & (row < 10)
    half = 2 * ((lane - 3 * BLK) // (2 * BLK)) + (inside >= BLK // 2).astype(jnp.int32)
    total = (lane >= 3 * BLK) & (half == row - (ROWS - SUMS))
    return jnp.where(quad | total, 1.0, 0.0).astype(B16)


def fold(first, second):
    low = lax.broadcasted_iota(jnp.int32, first.shape, 1) < BLK // 2
    return jnp.where(low, first, second) + pltpu.roll(jnp.where(low, second, first), BLK // 2, 1)


def forces_of(j, chooser, particles, sums, quads):
    parts = list(split3(quads[j]))
    for f in range(0, SUMS, 2):
        parts += split2(fold(sums[j, f], sums[j, f + 1]))
    mixed = contract(chooser, jnp.concatenate(parts, axis=1))
    qx, qy, qz, inner, xx, yy, zz, xy, yz, xz = (mixed[i : i + 1] for i in range(10))
    sx, sy, sz, pulls = (mixed[ROWS - SUMS + f : ROWS - SUMS + f + 1] for f in range(SUMS))
    x, y, z = (particles[f : f + 1, at_block(j)] for f in range(3))
    ax = xx * x + xy * y + xz * z
    ay = xy * x + yy * y + yz * z
    az = xz * x + yz * y + zz * z
    bent = ax * x + ay * y + az * z - 2 * (qx * x + qy * y + qz * z) + inner
    return (
        0.4 * (ax - qx) - sx,
        0.4 * (ay - qy) - sy,
        0.4 * (az - qz) - sz,
        -pulls - 0.2 * bent,
    )


def own_kernel(*refs):
    out, targets_out, spread_out = refs[4:7]
    (lists, list_counts, near_kept, near_counts, places, weights, near_places, fields, rows) = refs[7:16]
    targets, spread, sums, quads, sent, cell_lists, near_lists, particles, cells, arrived = refs[16:]
    copies = fetch(refs[:4], refs[21:25], arrived)
    blocks = cell_lists.shape[0]
    own_cells = cells.shape[1] // BLK
    clear(sums, quads)
    wait_for(copies)

    def by_field(b, unused):
        fields[pl.ds(b, 8, stride=own_cells), :] = cells[0:8, at_block(b)]
        fields[pl.ds(8 * own_cells + b, 2, stride=own_cells), :] = cells[8:10, at_block(b)]
        places[b] = cells[0:8, at_block(b)]
        return unused

    lax.fori_loop(0, own_cells, by_field, 0, unroll=16)

    def eight(g, unused):
        first = pl.multiple_of(8 * g, 8)
        x, y, z, _, xx, yy, _, xy, xz, yz = (
            fields[pl.ds(f * own_cells + first, 8), :] for f in range(10)
        )
        put_eight(first, quadrupole_rows(x, y, z, xx, yy, xy, xz, yz), rows)
        return unused

    lax.fori_loop(0, own_cells // 8, eight, 0, unroll=4)

    def step(b, unused):
        put_weights(b, rows, weights)
        return unused

    lax.fori_loop(0, own_cells, step, 0, unroll=16)
    weights[own_cells] = jnp.zeros((3 * ROWS, BLK), B16)
    places[own_cells] = jnp.zeros((8, BLK), F32)
    near_places[blocks] = jnp.zeros((8, BLK), F32)

    lane = lax.broadcasted_iota(jnp.int32, (BLK, BLK), 1)
    unit = jnp.where(lax.broadcasted_iota(jnp.int32, (BLK, BLK), 0) == lane, 1.0, 0.0).astype(B16)
    pick = coordinates()

    def prepare_target(j, unused):
        near_places[j, 0:4, :] = particles[:, at_block(j)]
        x, y, z = (wide(particles[f : f + 1, at_block(j)]) for f in range(3))
        high, middle, low = split3(target_rows(x, y, z))
        turned = contract(unit, jnp.concatenate([high, middle, low, high, middle, high], axis=0))
        turned = turned.astype(B16)
        targets[j] = turned
        begin_block(j, turned, pick, spread)
        return unused

    lax.fori_loop(0, blocks, prepare_target, 0, unroll=4)

    def make_lists(j):
        keep_some(
            j, lambda j, l: cell_lists[j, l], cell_lists.shape[1], 0, lists, list_counts,
            lambda b: (b < own_cells).astype(jnp.int32), own_cells,
        )
        keep_some(
            j, lambda j, l: near_lists[l, j], near_lists.shape[0], 0, near_kept, near_counts,
            lambda b: (b < blocks).astype(jnp.int32), blocks,
        )

    hand_on = fetch([targets, spread], [targets_out, spread_out], sent)
    add_all(
        blocks, make_lists, lists, list_counts, near_kept, near_counts, targets, spread, places, weights,
        near_places, sums, quads,
    )
    chooser = selectors()

    def finish_step(j, unused):
        for f, row in enumerate(forces_of(j, chooser, particles, sums, quads)):
            out[f : f + 1, at_block(j)] = row
        return unused

    lax.fori_loop(0, blocks, finish_step, 0, unroll=min(16, blocks))
    wait_for(hand_on)


def coordinates():
    shape = (6 * ROWS, 3 * BLK)
    row = lax.broadcasted_iota(jnp.int32, shape, 0)
    axis = lax.broadcasted_iota(jnp.int32, shape, 1) // BLK
    return jnp.where((row % ROWS == axis) & (row < 3 * ROWS), -0.5, 0.0).astype(B16)


def begin_block(j, turned, pick, spread):
    wider = jnp.dot(turned, pick, preferred_element_type=F32)
    for f in range(3):
        spread[j, f] = wider[:, f * BLK : (f + 1) * BLK]


def clear(sums, quads):
    def step(j, unused):
        for f in range(SUMS):
            sums[j, f] = jnp.zeros((BLK, BLK), F32)
        quads[j] = jnp.zeros((BLK, BLK), F32)
        return unused

    lax.fori_loop(0, quads.shape[0], step, 0)


def add_all(
    blocks, make_lists, lists, list_counts, near_kept, near_counts, targets, spread, places, weights,
    near_places, sums, quads,
):
    make_lists(0)

    def block_step(j, unused):
        add_block(
            j, list_counts[j], near_counts[j], lambda: make_lists(jnp.minimum(j + 1, blocks - 1)),
            lists, near_kept, targets, spread, places, weights, near_places, sums, quads,
        )
        return unused

    lax.fori_loop(0, blocks, block_step, 0)


def moved_kernel(own_cells, near_slots, *refs):
    out = refs[7]
    (lists, list_counts, near_kept, near_counts, places, weights, near_places, fields, rows) = refs[8:17]
    sums, quads, live = refs[17:20]
    cell_lists, near_lists, moved, particles, targets, spread, partial, arrived = refs[20:]
    copies = fetch(refs[:7], refs[20:27], arrived)
    blocks = cell_lists.shape[0]
    peers, slots = moved.shape[0], moved.shape[2]
    count = peers * slots
    near_moved = len(near_offsets) * near_slots
    me = lax.axis_index(("gx", "gy"))
    clear(sums, quads)

    def none_live(b, unused):
        live[b] = 0
        return unused

    lax.fori_loop(0, own_cells, none_live, 0, unroll=8)
    wait_for(copies[:3])

    def by_field(s, unused):
        for k in range(slots):
            b = s * slots + k
            fields[pl.ds(b, 4, stride=count), :] = moved[s, k]
            fields[pl.ds(4 * count + b, 4, stride=count), :] = moved[s, slots + k]
            places[b, 0:4, :] = moved[s, k]
        fields[pl.ds(8 * count + s * slots, slots), :] = moved[s, 2 * slots]
        return unused

    lax.fori_loop(0, peers, by_field, 0, unroll=8)

    bit = lax.broadcasted_iota(jnp.int32, (8, BLK), 0)

    def eight(g, unused):
        first = pl.multiple_of(8 * g, 8)
        x, y, z, mass, xx, yy, xz, xy, yz = (
            fields[pl.ds(f * count + first, 8), :] for f in range(9)
        )
        put_eight(first, quadrupole_rows(x, y, z, xx, yy, xy, xz, yz), rows)
        some = (mass != 0) | (xx != 0) | (yy != 0) | (xy != 0) | (xz != 0) | (yz != 0)
        some = jnp.max(jnp.where(some, 1.0, 0.0), axis=1, keepdims=True)
        code = jnp.sum(some * jnp.left_shift(1, bit[:, 0:1]).astype(F32)).astype(jnp.int32)
        for i in range(8):
            live[own_cells + first + i] = jnp.right_shift(code, i) & 1
        return unused

    lax.fori_loop(0, count // 8, eight, 0, unroll=8)
    weights[count] = jnp.zeros((3 * ROWS, BLK), B16)
    places[count] = jnp.zeros((8, BLK), F32)
    for position, offset in enumerate(near_offsets):
        source = me - offset
        there = (source >= 0) & (source < peers)
        safe = jnp.clip(source, 0, peers - 1)
        for k in range(near_slots):
            block = moved[safe, 2 * slots + 1 + k]
            near_places[position * near_slots + k, 0:4, :] = jnp.where(there, block, 0.0)
    near_places[near_moved] = jnp.zeros((8, BLK), F32)

    def step(b, unused):
        put_weights(b, rows, weights)
        return unused

    lax.fori_loop(0, count, step, 0, unroll=16)

    def make_lists(j):
        keep_some(
            j, lambda j, l: cell_lists[j, l], cell_lists.shape[1], own_cells, lists, list_counts,
            lambda b: live[b], count,
        )
        keep_some(
            j, lambda j, l: near_lists[l, j], near_lists.shape[0], blocks, near_kept, near_counts,
            lambda b: (b >= blocks).astype(jnp.int32), near_moved,
        )

    wait_for(copies[3:])
    add_all(
        blocks, make_lists, lists, list_counts, near_kept, near_counts, targets, spread, places, weights,
        near_places, sums, quads,
    )

    chooser = selectors()

    def finish_step(j, unused):
        for f, row in enumerate(forces_of(j, chooser, particles, sums, quads)):
            out[f : f + 1, at_block(j)] = row + partial[f : f + 1, at_block(j)]
        return unused

    lax.fori_loop(0, blocks, finish_step, 0, unroll=min(16, blocks))


def scratch(blocks, cells, near, list_width, near_width):
    return [
        pltpu.SMEM((blocks, list_width + 4), jnp.int32),
        pltpu.SMEM((blocks,), jnp.int32),
        pltpu.SMEM((blocks, near_width + 4), jnp.int32),
        pltpu.SMEM((blocks,), jnp.int32),
        pltpu.VMEM((cells + 1, 8, BLK), F32),
        pltpu.VMEM((cells + 1, 3 * ROWS, BLK), B16),
        pltpu.VMEM((near + 1, 8, BLK), F32),
        pltpu.VMEM((16 * cells, BLK), F32),
        pltpu.VMEM((ROWS * (cells + 8), BLK), F32),
    ]


def body(particles, tree_cells, let_list, let_count, part_list, cell_lists, near_lists):
    peers = lax.axis_size(("gx", "gy"))
    slots = let_list.shape[2]
    near_slots = part_list.shape[2]
    blocks, list_width = cell_lists.shape
    near_width = near_lists.shape[1]
    own_cells = tree_cells.shape[1] // BLK
    far = pl.BlockSpec(memory_space=pltpu.HBM)
    vmem = pl.BlockSpec(memory_space=pltpu.VMEM)
    params = pltpu.CompilerParams(vmem_limit_bytes=60 * 2**20)

    def landing(numbers, arrays):
        spaces = [pltpu.SMEM(a.shape, a.dtype) for a in numbers]
        spaces += [pltpu.VMEM(a.shape, a.dtype) for a in arrays]
        return spaces + [pltpu.SemaphoreType.DMA((len(spaces),))]

    choice = [jnp.transpose(let_list[0]), let_count, part_list[0]]
    chosen = pl.pallas_call(
        pick_kernel,
        out_shape=jax.ShapeDtypeStruct((peers, 2 * slots + 1 + near_slots, 4, BLK), F32),
        in_specs=[far] * 5,
        out_specs=far,
        scratch_shapes=[
            pltpu.VMEM((peers, 2 * slots + 1 + near_slots, 4, BLK), F32),
            pltpu.SemaphoreType.DMA((4,)),
        ]
        + landing(choice, [tree_cells, particles]),
        compiler_params=params,
    )(*choice, tree_cells, particles)
    moved = lax.all_to_all(chosen, ("gx", "gy"), split_axis=0, concat_axis=0, tiled=True)

    numbers = [cell_lists, jnp.transpose(near_lists)]
    turned = [
        jax.ShapeDtypeStruct((blocks, BLK, 6 * ROWS), B16),
        jax.ShapeDtypeStruct((blocks, 3, BLK, BLK), F32),
    ]
    sums = [pltpu.VMEM((blocks, SUMS, BLK, BLK), F32), pltpu.VMEM((blocks, BLK, BLK), F32)]
    partial, *turned = pl.pallas_call(
        own_kernel,
        out_shape=[jax.ShapeDtypeStruct(particles.shape, F32)] + turned,
        in_specs=[far] * 4,
        out_specs=[vmem, far, far],
        scratch_shapes=scratch(blocks, own_cells, blocks, list_width, near_width)
        + [pltpu.VMEM(leaf.shape, leaf.dtype) for leaf in turned]
        + sums
        + [pltpu.SemaphoreType.DMA((2,))]
        + landing(numbers, [particles, tree_cells]),
        compiler_params=pltpu.CompilerParams(vmem_limit_bytes=127 * 2**19),
        cost_estimate=pl.CostEstimate(flops=10**9, bytes_accessed=10**6, transcendentals=10**6),
    )(*numbers, particles, tree_cells)

    return pl.pallas_call(
        functools.partial(moved_kernel, own_cells, near_slots),
        out_shape=jax.ShapeDtypeStruct(particles.shape, F32),
        in_specs=[far] * 7,
        out_specs=vmem,
        scratch_shapes=scratch(
            blocks, peers * slots, len(near_offsets) * near_slots, list_width, near_width
        )
        + sums
        + [pltpu.SMEM((own_cells + peers * slots,), jnp.int32)]
        + landing(numbers, [moved, particles, *turned, partial]),
        compiler_params=params,
    )(*numbers, moved, particles, *turned, partial)


def solution(mesh):
    return jax.shard_map(
        body,
        mesh=mesh,
        in_specs=(
            P(None, ("gx", "gy")),
            P(None, ("gx", "gy")),
            P(("gx", "gy"), None, None),
            P(("gx", "gy"), None),
            P(("gx", "gy"), None, None),
            P(("gx", "gy"), None),
            P(("gx", "gy"), None),
        ),
        out_specs=P(None, ("gx", "gy")),
        check_vma=False,
    )
```
